32 devices in a mesh: ctx: 8 (over z, x), tensor: 4 (over y, core).
Axes of the slice: x: 2, y: 2, z: 4, core: 2. Of those that a mesh axis runs over, the one named last changes fastest.
Arguments:
- queries: bfloat16 [3072, 8192], P('ctx', 'tensor'), may hold values from -64 to 64
- key_layout_rows: bfloat16 [3072, 1024], P('ctx', 'tensor'), may hold values from -5 to 5
- value_layout_rows: bfloat16 [3072, 1024], P('ctx', 'tensor'), may hold values from -6 to 6
- output_gradient: bfloat16 [3072, 8192], P('ctx', 'tensor'), may hold values from -6 to 6
- doc_starts: int32 [24], P('ctx'), may hold values from 0 to 1, as said below
- block_mapping: int32 [24], replicated, may hold values from 0 to 23, as said below
Outputs:
- query_grad: bfloat16 [3072, 8192], P(('ctx', 'tensor'))
- key_grad: bfloat16 [3072, 1024], P(('ctx', 'tensor'))
- value_grad: bfloat16 [3072, 1024], P(('ctx', 'tensor'))
The draws below stay inside these ranges and needn't reach their ends.
Inputs may be any that keep to these rules, and one draw needn't show every extreme that they name: `doc_starts`: the first block of every index of ctx begins a document, so in the executing layout every document lies whole within the 384 tokens of one index of ctx. A permutation of the blocks. Block s lies on index s // 3 of ctx; block_mapping[s] lies on that index or on the index 4 away. At least one and at most 2 blocks of each index come from the other index of its pair; indices 0 and 4 take exactly 2.
All inputs are finite; a program needn't handle non-finite values.
Results may differ from the reference program's by a relative error of at most 0.006.
Values may be sent and summed in bfloat16 or wider, within the bound.
No kernel may reach another device: no remote copies, remote signals or barrier semaphores. Data moves between devices by JAX's collectives and lax.ppermute only.
A program may use at most 64 MiB of HBM per device.

```python
import jax
import jax.numpy as jnp
from jax import lax

QUERY_HEADS = 64
KEY_VALUE_HEADS = 8
HEAD_SIZE = 128
TOKENS_PER_SHARD = 384
BLK = 128
NBLK = 3
CAP = 2
TOKEN_COUNT = 3072
NBLOCKS = 24
N_CTX = 8


def draw_key_layout_rows(key, part):
    drawn = jax.random.normal(jax.random.fold_in(key, 101), (TOKEN_COUNT, KEY_VALUE_HEADS * HEAD_SIZE), jnp.float32)
    return jnp.clip(drawn, -5.0, 5.0).astype(jnp.bfloat16)


def draw_queries(key, part):
    drawn = jax.random.normal(jax.random.fold_in(key, 102), (TOKEN_COUNT, QUERY_HEADS * HEAD_SIZE), jnp.float32)
    return jnp.clip(drawn, -5.0, 5.0).astype(jnp.bfloat16)


def draw_doc_starts(key, part):
    flags = jax.random.randint(jax.random.fold_in(key, 7), (N_CTX, NBLK), 0, 2, jnp.int32)
    flags = flags.at[:, 0].set(1)
    return flags.reshape(NBLOCKS).astype(jnp.int32)


def draw_block_mapping(key, part):
    half_axis = N_CTX // 2
    moved_counts = jax.random.randint(jax.random.fold_in(key, 12), (half_axis,), 1, CAP + 1, jnp.int32)
    moved_counts = moved_counts.at[0].set(CAP)
    pair_keys = jax.random.split(jax.random.fold_in(key, 11), half_axis)

    def one_pair(pair_key, moved, first):
        key_one, key_two, key_three, key_four = jax.random.split(pair_key, 4)
        order_first = jax.random.permutation(key_one, NBLK).astype(jnp.int32)
        order_second = jax.random.permutation(key_two, NBLK).astype(jnp.int32)
        slot_ids = jnp.arange(NBLK, dtype=jnp.int32)
        base_first = first * NBLK
        base_second = (first + half_axis) * NBLK
        takes_first = jnp.where(slot_ids < moved, base_second + order_second, base_first + order_first)
        takes_second = jnp.where(slot_ids < moved, base_first + order_first, base_second + order_second)
        shuffle_first = jax.random.permutation(key_three, NBLK)
        shuffle_second = jax.random.permutation(key_four, NBLK)
        return (takes_first[shuffle_first], takes_second[shuffle_second])
    rows_first, rows_second = jax.vmap(one_pair)(pair_keys, moved_counts, jnp.arange(half_axis, dtype=jnp.int32))
    return jnp.concatenate([rows_first, rows_second], axis=0).reshape(NBLOCKS).astype(jnp.int32)


def level_of(stream_key, shape, shards, least, largest):
    factor_of = 1.0
    for dim, parts in shards:
        steps = jax.random.uniform(jax.random.fold_in(jax.random.fold_in(stream_key, 6), dim), (parts,), jnp.float32, least / len(shards), largest / len(shards))
        factor_of = factor_of * jnp.repeat(jnp.exp(steps), shape[dim] // parts).reshape((-1,) + (1,) * (len(shape) - 1 - dim))
    return factor_of


def noise(rng, extent, spread, limit, cuts=(), held_as=jnp.bfloat16):
    entries = spread * jax.random.normal(rng, extent, jnp.float32)
    if cuts:
        entries = entries * level_of(rng, extent, cuts, -0.22, 0.18)
    return jnp.clip(entries, -limit, limit).astype(held_as)


def setup_inputs(seed: int = 0) -> dict:
    key_list = jax.random.split(jax.random.key(seed), 7)
    return {
        "queries": draw_queries(jax.random.fold_in(key_list[6], 71), 0),
        "key_layout_rows": draw_key_layout_rows(jax.random.fold_in(key_list[6], 71), 0),
        "value_layout_rows": noise(key_list[2], (TOKEN_COUNT, KEY_VALUE_HEADS * HEAD_SIZE), 1.0, 6.0, ((0, 8), (1, 4))),
        "output_gradient": noise(key_list[3], (TOKEN_COUNT, QUERY_HEADS * HEAD_SIZE), 1.0, 6.0, ((0, 8), (1, 4))),
        "doc_starts": draw_doc_starts(jax.random.fold_in(key_list[6], 71), 0),
        "block_mapping": draw_block_mapping(jax.random.fold_in(key_list[6], 71), 0),
    }


def rounded(values):
    return lax.optimization_barrier(values.astype(jnp.bfloat16)).astype(jnp.float32)


def device_grads(inputs):
    queries, key_layout_rows, value_layout_rows, output_gradient, starts = inputs
    head_repeats = QUERY_HEADS // KEY_VALUE_HEADS
    scaling = HEAD_SIZE ** -0.5
    document = jnp.repeat(jnp.cumsum(starts).astype(jnp.int32), BLK)
    position = jnp.arange(TOKENS_PER_SHARD, dtype=jnp.int32)
    visible = (document[:, None] == document[None, :]) & (position[:, None] >= position[None, :])
    query_expanded = queries.astype(jnp.float32).reshape(TOKENS_PER_SHARD, KEY_VALUE_HEADS, head_repeats, HEAD_SIZE)
    gradient_expanded = output_gradient.astype(jnp.float32).reshape(TOKENS_PER_SHARD, KEY_VALUE_HEADS, head_repeats, HEAD_SIZE)
    key_expanded = key_layout_rows.astype(jnp.float32).reshape(TOKENS_PER_SHARD, KEY_VALUE_HEADS, HEAD_SIZE)
    value_expanded = value_layout_rows.astype(jnp.float32).reshape(TOKENS_PER_SHARD, KEY_VALUE_HEADS, HEAD_SIZE)
    scores = jnp.einsum("qgrd,kgd->grqk", query_expanded, key_expanded) * scaling
    row_top = jnp.max(jnp.where(visible, scores, -1e30), axis=-1, keepdims=True)
    weights = jnp.where(visible, jnp.exp(scores - row_top), 0.0)
    weights = weights / jnp.sum(weights, axis=-1, keepdims=True)
    dprobs = jnp.einsum("qgrd,kgd->grqk", gradient_expanded, value_expanded)
    row_delta = jnp.sum(weights * dprobs, axis=-1, keepdims=True)
    value_running = jnp.einsum("grqk,qgrd->kgd", rounded(weights), gradient_expanded)
    dscores = rounded(weights * (dprobs - row_delta))
    query_exec = jnp.einsum("grqk,kgd->qgrd", dscores, key_expanded) * scaling
    key_running = jnp.einsum("grqk,qgrd->kgd", dscores, query_expanded) * scaling
    return (query_exec.reshape(TOKENS_PER_SHARD, QUERY_HEADS * HEAD_SIZE).astype(jnp.bfloat16),
            key_running.reshape(TOKENS_PER_SHARD, KEY_VALUE_HEADS * HEAD_SIZE).astype(jnp.bfloat16),
            value_running.reshape(TOKENS_PER_SHARD, KEY_VALUE_HEADS * HEAD_SIZE).astype(jnp.bfloat16))


def return_to_owner(gradients, block_mapping):
    columns = gradients.shape[-1]
    blocks = gradients.reshape(NBLOCKS, BLK, columns)
    owned = jnp.zeros_like(blocks).at[block_mapping].set(blocks)
    return owned.reshape(TOKEN_COUNT, columns)


def reference(queries, key_layout_rows, value_layout_rows, output_gradient, doc_starts, block_mapping):
    stacked = (queries.reshape(N_CTX, TOKENS_PER_SHARD, QUERY_HEADS * HEAD_SIZE),
               key_layout_rows.reshape(N_CTX, TOKENS_PER_SHARD, KEY_VALUE_HEADS * HEAD_SIZE),
               value_layout_rows.reshape(N_CTX, TOKENS_PER_SHARD, KEY_VALUE_HEADS * HEAD_SIZE),
               output_gradient.reshape(N_CTX, TOKENS_PER_SHARD, QUERY_HEADS * HEAD_SIZE),
               doc_starts.reshape(N_CTX, NBLK))
    query_exec, key_running, value_running = lax.map(device_grads, stacked)
    return (return_to_owner(query_exec.reshape(TOKEN_COUNT, QUERY_HEADS * HEAD_SIZE), block_mapping),
            return_to_owner(key_running.reshape(TOKEN_COUNT, KEY_VALUE_HEADS * HEAD_SIZE), block_mapping),
            return_to_owner(value_running.reshape(TOKEN_COUNT, KEY_VALUE_HEADS * HEAD_SIZE), block_mapping))
```

```python
import functools
import math

import jax
import jax.numpy as jnp
from jax import lax
from jax.experimental import pallas as pl
from jax.experimental.pallas import tpu as pltpu
from jax.sharding import PartitionSpec as P

HEAD_SIZE = 128
CAP = 2
HIDDEN = -1e30
VMEM_LIMIT = 60 * 1024 * 1024
KEYS_AND_VALUES = -1
PACK = 4
NO_COST = pl.CostEstimate(flops=1000, bytes_accessed=1000, transcendentals=0)
PARAMS = pltpu.CompilerParams(vmem_limit_bytes=VMEM_LIMIT)
IN_SMEM = pl.BlockSpec(memory_space=pltpu.SMEM)
IN_VMEM = pl.BlockSpec(memory_space=pltpu.VMEM)
ANYWHERE = pl.BlockSpec(memory_space=pl.ANY)


def contract(a, b, dims):
    return lax.dot_general(a, b, ((dims[:1], dims[1:]), ((), ())), preferred_element_type=jnp.float32)


def aligned(start, size, step):
    return pl.ds(pl.multiple_of(start, step), size)


def own_sources(mapping_ref, position, block_count):
    sources = [jnp.int32(-1)] * block_count
    for block in range(block_count):
        target = mapping_ref[position * block_count + block] - position * block_count
        for slot in range(block_count):
            sources[slot] = jnp.where(target == slot, block, sources[slot])
    return sources


def moved_blocks(mapping_ref, position, block_count):
    moved = [jnp.int32(0)] * CAP
    seen = jnp.int32(0)
    for block in range(block_count):
        target = mapping_ref[position * block_count + block] - position * block_count
        leaves = (target < 0) | (target >= block_count)
        for slot in range(CAP):
            moved[slot] = jnp.where(leaves & (seen <= slot), block, moved[slot])
        seen = seen + jnp.where(leaves, 1, 0)
    return moved


def heads_gradients(q_ref, g_ref, k_ref, v_ref, bias_ref, columns, block_count, block_rows):
    rate = HEAD_SIZE ** (-0.5) * math.log2(math.e)
    weights_low, dscores, query_pieces = [], [], []
    for block in range(block_count):
        rows = slice(block * block_rows, (block + 1) * block_rows)
        width = (block + 1) * block_rows
        q = jnp.concatenate([q_ref[rows, c] for c in columns], axis=0)
        g = jnp.concatenate([g_ref[rows, c] for c in columns], axis=0)
        k, v = k_ref[:width, :], v_ref[:width, :]
        bias = jnp.concatenate([bias_ref[:width, rows]] * len(columns), axis=1)
        scores = contract(k, q, (1, 1)) + bias
        top = jnp.max(scores, axis=0, keepdims=True)
        weights = jnp.exp2((scores - top) * rate)
        dprobs = contract(v, g, (1, 1))
        share = 1.0 / jnp.sum(weights, axis=0, keepdims=True)
        delta = jnp.sum(weights * dprobs, axis=0, keepdims=True) * share
        weights = weights * share
        weights_low.append(weights.astype(jnp.bfloat16))
        dscores.append((weights * (dprobs - delta)).astype(jnp.bfloat16))
        query_pieces.append((contract(dscores[-1], k, (0, 0)) * HEAD_SIZE ** (-0.5)).astype(jnp.bfloat16))
    return query_pieces, dscores, weights_low


def grads_kernel(block_count, block_rows, first, last, heads, sets, *refs):
    position_ref, starts_ref, mapping_ref, q_ref, g_ref, k_ref, v_ref, _, *refs = refs
    if not first:
        key_in, value_in, *refs = refs
    outs, refs = refs[: 2 * len(sets)], refs[2 * len(sets) :]
    if not last:
        key_out, value_out, *refs = refs
    bias_ref, low_ref, key_acc, value_acc = refs
    position = position_ref[0]
    rows = block_count * block_rows

    document_row = jnp.int32(0)
    for block in range(block_count):
        document_row = jnp.where(starts_ref[block] != 0, block * block_rows, document_row)
        width = (block + 1) * block_rows
        at_key = lax.broadcasted_iota(jnp.int32, (width, block_rows), 0)
        at_row = lax.broadcasted_iota(jnp.int32, (width, block_rows), 1) + block * block_rows
        visible = (at_key <= at_row) & (at_key >= document_row)
        bias_ref[:width, block * block_rows : width] = jnp.where(visible, 0.0, HIDDEN)
    if first:
        key_acc[...] = jnp.zeros_like(key_acc)
        value_acc[...] = jnp.zeros_like(value_acc)
    else:
        key_acc[...] = key_in[...]
        value_acc[...] = value_in[...]

    owned = [jnp.maximum(source, 0) for source in own_sources(mapping_ref, position, block_count)]
    moved = moved_blocks(mapping_ref, position, block_count)

    def put(own_ref, send_ref, at):
        columns = slice(at * HEAD_SIZE, (at + 1) * HEAD_SIZE)
        for slot, source in enumerate(owned):
            own_ref[slot * block_rows : (slot + 1) * block_rows, columns] = low_ref[
                aligned(source * block_rows, block_rows, block_rows), :
            ]
        for slot, source in enumerate(moved):
            send_ref[slot * block_rows : (slot + 1) * block_rows, columns] = low_ref[
                aligned(source * block_rows, block_rows, block_rows), :
            ]

    places = {unit: (outs[2 * i], outs[2 * i + 1], at) for i, units in enumerate(sets) for at, unit in enumerate(units)}
    for head in range(0, heads, PACK):
        packed = range(head, min(head + PACK, heads))
        columns = [slice(h * HEAD_SIZE, (h + 1) * HEAD_SIZE) for h in packed]
        query_pieces, dscores, weights_low = heads_gradients(
            q_ref, g_ref, k_ref, v_ref, bias_ref, columns, block_count, block_rows
        )
        stacked = lambda ref, block: [ref[b * block_rows : (b + 1) * block_rows, c] for b in range(block, block_count) for c in columns]
        for block in range(block_count):
            seen = slice(block * block_rows, (block + 1) * block_rows)
            joined = lambda pieces: jnp.concatenate([p[seen, :] for p in pieces[block:]], axis=1)
            value_acc[seen, :] += contract(joined(weights_low), jnp.concatenate(stacked(g_ref, block), axis=0), (1, 0))
            key_acc[seen, :] += contract(joined(dscores), jnp.concatenate(stacked(q_ref, block), axis=0), (1, 0))
        for index, h in enumerate(packed):
            for block in range(block_count):
                low_ref[block * block_rows : (block + 1) * block_rows, :] = query_pieces[block][
                    index * block_rows : (index + 1) * block_rows, :
                ]
            put(*places[h])
    if last:
        own_ref, send_ref, at = places[KEYS_AND_VALUES]
        low_ref[...] = (key_acc[...] * HEAD_SIZE ** (-0.5)).astype(jnp.bfloat16)
        put(own_ref, send_ref, at)
        low_ref[...] = value_acc[...].astype(jnp.bfloat16)
        put(own_ref, send_ref, at + 1)
    else:
        key_out[...] = key_acc[...]
        value_out[...] = value_acc[...]


def unit_columns(units):
    return (len(units) + units.count(KEYS_AND_VALUES)) * HEAD_SIZE


def grads_chunk(
    position, starts, mapping, queries, gradient, keys, values, after, carried, start_head, heads, group, sets
):
    rows = queries.shape[0]
    block_count = starts.shape[0]
    block_rows = rows // block_count
    first = carried is None
    last = any(KEYS_AND_VALUES in units for units in sets)
    whole = lambda r, c: pl.BlockSpec((r, c), lambda i: (0, 0))
    cut = pl.BlockSpec((pl.Element(rows), pl.Element(heads * HEAD_SIZE)), lambda i: (0, start_head * HEAD_SIZE))
    group_spec = pl.BlockSpec((rows, HEAD_SIZE), lambda i: (0, group))
    running = jax.ShapeDtypeStruct((rows, HEAD_SIZE), jnp.float32)
    out_shape = []
    for units in sets:
        out_shape.append(jax.ShapeDtypeStruct((rows, unit_columns(units)), jnp.bfloat16))
        out_shape.append(jax.ShapeDtypeStruct((CAP * block_rows, unit_columns(units)), jnp.bfloat16))
    if not last:
        out_shape += [running, running]
    out = pl.pallas_call(
        functools.partial(grads_kernel, block_count, block_rows, first, last, heads, sets),
        grid=(1,),
        in_specs=[IN_SMEM] * 3
        + [cut, cut, group_spec, group_spec, ANYWHERE]
        + ([] if first else [whole(rows, HEAD_SIZE)] * 2),
        out_specs=[whole(*s.shape) for s in out_shape],
        out_shape=out_shape,
        scratch_shapes=[
            pltpu.VMEM((rows, rows), jnp.float32),
            pltpu.VMEM((rows, HEAD_SIZE), jnp.bfloat16),
            pltpu.VMEM((rows, HEAD_SIZE), jnp.float32),
            pltpu.VMEM((rows, HEAD_SIZE), jnp.float32),
        ],
        compiler_params=PARAMS,
        cost_estimate=NO_COST,
    )(position, starts, mapping, queries, gradient, keys, values, after, *(carried or ()))
    pairs = [(out[2 * i], out[2 * i + 1]) for i in range(len(sets))]
    return pairs, (None if last else tuple(out[2 * len(sets) :]))


def sort_kernel(block_count, block_rows, half_axis, peers, position_ref, mapping_ref, own_ref, arrived_ref, *refs):
    outs = refs[-peers:]
    at, peer = position_ref[0], position_ref[1]
    partner = lax.rem(at + half_axis, 2 * half_axis)
    arrived_slot = [jnp.int32(-1)] * block_count
    for index, block in enumerate(moved_blocks(mapping_ref, partner, block_count)):
        target = mapping_ref[partner * block_count + block] - at * block_count
        for slot in range(block_count):
            arrived_slot[slot] = jnp.where(target == slot, index, arrived_slot[slot])
    share = block_count * block_rows // peers
    step = math.gcd(share, block_rows)
    for hop, out_ref in enumerate(outs):
        to_peer = jnp.bitwise_xor(peer, hop)
        for piece in range(share // step):
            row = to_peer * share + piece * step
            block = lax.div(row, block_rows)
            slot = jnp.int32(-1)
            for b in range(block_count):
                slot = jnp.where(block == b, arrived_slot[b], slot)
            from_own = own_ref[aligned(row, step, step), :]
            from_pair = arrived_ref[
                aligned(jnp.maximum(slot, 0) * block_rows + lax.rem(row, block_rows), step, step), :
            ]
            out_ref[piece * step : (piece + 1) * step, :] = jnp.where(slot >= 0, from_pair, from_own)


def sort_rows(position, mapping, own, arrived, after, block_count, half_axis, peers):
    rows, columns = own.shape
    out = jax.ShapeDtypeStruct((rows // peers, columns), own.dtype)
    return pl.pallas_call(
        functools.partial(sort_kernel, block_count, rows // block_count, half_axis, peers),
        in_specs=[IN_SMEM, IN_SMEM, IN_VMEM, IN_VMEM] + [ANYWHERE] * len(after),
        out_specs=[IN_VMEM] * peers,
        out_shape=[out] * peers,
        compiler_params=PARAMS,
        cost_estimate=NO_COST,
    )(position, mapping, own, arrived, *after)


def place_kernel(peers, columns_here, places, held, position_ref, *refs):
    pieces = refs[: peers * len(places)]
    outs, sem = refs[-len(columns_here) - 1 : -1], refs[-1]
    peer = position_ref[1]
    copies = []
    for index, parts in enumerate(places):
        for hop in range(peers):
            from_peer = jnp.bitwise_xor(peer, hop)
            piece = pieces[index * peers + hop]
            for at, size, out, column in parts:
                copies.append(
                    pltpu.make_async_copy(
                        piece.at[:, at : at + size],
                        outs[out].at[:, aligned(from_peer * columns_here[out] + column, size, HEAD_SIZE)],
                        sem.at[len(copies)],
                    )
                )
                copies[-1].start()
    for copy in copies:
        copy.wait()


def place_columns(position, pieces, places, columns_here, held, peers):
    rows = pieces[0][0].shape[0]
    flat = [p for chunk in pieces for p in chunk]
    count = peers * sum(len(parts) for parts in places)
    out_shape = [jax.ShapeDtypeStruct((rows, peers * c), pieces[0][0].dtype) for c in columns_here]
    return pl.pallas_call(
        functools.partial(place_kernel, peers, columns_here, places, len(held)),
        in_specs=[IN_SMEM] + [IN_VMEM] * len(flat) + [ANYWHERE] * len(held),
        out_specs=[ANYWHERE] * len(out_shape),
        out_shape=out_shape,
        input_output_aliases={1 + len(flat) + i: i for i in range(len(held))},
        scratch_shapes=[pltpu.SemaphoreType.DMA((count,))],
        compiler_params=PARAMS,
        cost_estimate=NO_COST,
    )(position, *flat, *held)


def plan_of(groups, repeats):
    lead, most = max(1, repeats // 2), max(1, 3 * repeats // 4)
    kernels = [(0, 0, lead, [list(range(lead))])]
    kernels.append((0, lead, repeats - lead, [list(range(repeats - lead)) + [KEYS_AND_VALUES]]))
    for group in range(1, groups):
        heads = list(range(repeats))
        kernels.append((group, 0, repeats, [heads[:most], heads[most:] + [KEYS_AND_VALUES]]))
    return kernels


def on_device(queries, key_layout_rows, value_layout_rows, output_gradient, doc_starts, block_mapping):
    rows = queries.shape[0]
    block_count = doc_starts.shape[0]
    groups = key_layout_rows.shape[1] // HEAD_SIZE
    repeats = queries.shape[1] // key_layout_rows.shape[1]
    axis_length = lax.axis_size("ctx")
    half_axis = axis_length // 2
    peers = lax.axis_size("tensor")
    position = jnp.stack([lax.axis_index("ctx"), lax.axis_index("tensor")]).astype(jnp.int32)
    pairs = [(i, (i + half_axis) % axis_length) for i in range(axis_length)]

    carried, after, sent = None, key_layout_rows, []
    for group, start, heads, sets in plan_of(groups, repeats):
        made, carried = grads_chunk(
            position, doc_starts, block_mapping, queries, output_gradient, key_layout_rows, value_layout_rows,
            after, carried, group * repeats + start, heads, group, sets,
        )
        after = made[0][0]
        for units, (own, send) in zip(sets, made):
            sent.append((group, start, units, own, lax.ppermute(send, "ctx", pairs)))

    order, pieces, places = [after], [], []
    for group, start, units, own, arrived in sent:

        def exchange(own, arrived, *order):
            parts = sort_rows(position, block_mapping, own, arrived, order, block_count, half_axis, peers)
            return [parts[0]] + [
                lax.ppermute(parts[hop], "tensor", [(i, i ^ hop) for i in range(peers)]) for hop in range(1, peers)
            ]

        def nothing(own, arrived, *order):
            return [jnp.zeros((rows // peers, own.shape[1]), own.dtype)] * peers

        if len(pieces) < len(sent) - 1:
            got = lax.cond(block_mapping[0] >= 0, exchange, nothing, own, arrived, *order)
        else:
            got = exchange(own, arrived, *order)
        order = [got[0]]
        pieces.append(got)
        parts, at = [], 0
        queries_here = [u for u in units if u != KEYS_AND_VALUES]
        if queries_here:
            size = len(queries_here) * HEAD_SIZE
            parts.append((0, size, 0, (group * repeats + start + queries_here[0]) * HEAD_SIZE))
            at = size
        if KEYS_AND_VALUES in units:
            parts.append((at, HEAD_SIZE, 1, group * HEAD_SIZE))
            parts.append((at + HEAD_SIZE, HEAD_SIZE, 2, group * HEAD_SIZE))
        places.append(parts)
    columns_here = [queries.shape[1], key_layout_rows.shape[1], value_layout_rows.shape[1]]
    held = []
    if len(pieces) > 1:
        held = place_columns(position, pieces[:-1], places[:-1], columns_here, [], peers)
    return tuple(place_columns(position, pieces[-1:], places[-1:], columns_here, held, peers))


def solution(mesh):
    return jax.shard_map(
        on_device,
        mesh=mesh,
        in_specs=(
            P("ctx", "tensor"),
            P("ctx", "tensor"),
            P("ctx", "tensor"),
            P("ctx", "tensor"),
            P("ctx"),
            P(),
        ),
        out_specs=(
            P(("ctx", "tensor"), None),
            P(("ctx", "tensor"), None),
            P(("ctx", "tensor"), None),
        ),
        check_vma=False,
    )
```

```python
import functools
import math

import jax
import jax.numpy as jnp
from jax import lax
from jax.experimental import pallas as pl
from jax.experimental.pallas import tpu as pltpu
from jax.sharding import PartitionSpec as P

HEAD_SIZE = 128
CAP = 2
HIDDEN = -1e30
FULL_VMEM, SOME_VMEM, LITTLE_VMEM = (60 << 20, 30 << 20, 8 << 20)
PACK = 4
NO_COST = pl.CostEstimate(flops=1000, bytes_accessed=1000, transcendentals=0)
IN_SMEM = pl.BlockSpec(memory_space=pltpu.SMEM)
IN_VMEM = pl.BlockSpec(memory_space=pltpu.VMEM)
ANYWHERE = pl.BlockSpec(memory_space=pl.ANY)


def contract(a, b, dims):
    return lax.dot_general(a, b, ((dims[:1], dims[1:]), ((), ())), preferred_element_type=jnp.float32)


def aligned(start, size, step):
    return pl.ds(pl.multiple_of(start, step), size)


def own_sources(mapping_ref, position, block_count):
    sources = [jnp.int32(-1)] * block_count
    for block in range(block_count):
        target = mapping_ref[position * block_count + block] - position * block_count
        for slot in range(block_count):
            sources[slot] = jnp.where(target == slot, block, sources[slot])
    return sources


def moved_blocks(mapping_ref, position, block_count):
    moved = [jnp.int32(0)] * CAP
    seen = jnp.int32(0)
    for block in range(block_count):
        target = mapping_ref[position * block_count + block] - position * block_count
        leaves = (target < 0) | (target >= block_count)
        for slot in range(CAP):
            moved[slot] = jnp.where(leaves & (seen <= slot), block, moved[slot])
        seen = seen + jnp.where(leaves, 1, 0)
    return moved


def heads_gradients(q_ref, g_ref, k_ref, v_ref, bias_ref, columns, block_count, block_rows):
    rate = HEAD_SIZE ** (-0.5) * math.log2(math.e)
    weights_low, dscores, query_pieces = [], [], []
    for block in range(block_count):
        rows = slice(block * block_rows, (block + 1) * block_rows)
        width = (block + 1) * block_rows
        q = jnp.concatenate([q_ref[rows, c] for c in columns], axis=0)
        g = jnp.concatenate([g_ref[rows, c] for c in columns], axis=0)
        k, v = k_ref[:width, :], v_ref[:width, :]
        bias = jnp.concatenate([bias_ref[:width, rows]] * len(columns), axis=1)
        scores = contract(k, q, (1, 1)) + bias
        top = jnp.max(scores, axis=0, keepdims=True)
        weights = jnp.exp2((scores - top) * rate)
        dprobs = contract(v, g, (1, 1))
        share = 1.0 / jnp.sum(weights, axis=0, keepdims=True)
        delta = jnp.sum(weights * dprobs, axis=0, keepdims=True) * share
        weights = weights * share
        weights_low.append(weights.astype(jnp.bfloat16))
        dscores.append((weights * (dprobs - delta)).astype(jnp.bfloat16))
        query_pieces.append((contract(dscores[-1], k, (0, 0)) * HEAD_SIZE ** (-0.5)).astype(jnp.bfloat16))
    return query_pieces, dscores, weights_low


def pairs_of(refs):
    return list(zip(refs[::2], refs[1::2]))


def grads_kernel(block_count, block_rows, group, first, keeps, held, heads, sets, *refs):
    starts_ref, mapping_ref, q_ref, g_ref, k_ref, v_ref, _, *refs = refs
    sums, refs = dict(zip(held, pairs_of(refs[: 2 * len(held)]))), refs[2 * len(held) :]
    outs, refs = pairs_of(refs[: 2 * len(sets)]), refs[2 * len(sets) :]
    if keeps:
        key_out, value_out, *refs = refs
    bias_ref, low_ref, key_acc, value_acc = refs
    position = lax.axis_index("ctx")
    rows = block_count * block_rows

    document_row = jnp.int32(0)
    for block in range(block_count):
        document_row = jnp.where(starts_ref[block] != 0, block * block_rows, document_row)
        width = (block + 1) * block_rows
        at_key = lax.broadcasted_iota(jnp.int32, (width, block_rows), 0)
        at_row = lax.broadcasted_iota(jnp.int32, (width, block_rows), 1) + block * block_rows
        visible = (at_key <= at_row) & (at_key >= document_row)
        bias_ref[:width, block * block_rows : width] = jnp.where(visible, 0.0, HIDDEN)
    if first:
        key_acc[...] = jnp.zeros_like(key_acc)
        value_acc[...] = jnp.zeros_like(value_acc)
    else:
        key_acc[...] = sums[group][0][...]
        value_acc[...] = sums[group][1][...]
    sums[group] = (key_acc, value_acc)

    owned = [jnp.maximum(source, 0) for source in own_sources(mapping_ref, position, block_count)]
    moved = moved_blocks(mapping_ref, position, block_count)

    def put(own_ref, send_ref, at):
        columns = slice(at * HEAD_SIZE, (at + 1) * HEAD_SIZE)
        for slot, source in enumerate(owned):
            own_ref[slot * block_rows : (slot + 1) * block_rows, columns] = low_ref[
                aligned(source * block_rows, block_rows, block_rows), :
            ]
        for slot, source in enumerate(moved):
            send_ref[slot * block_rows : (slot + 1) * block_rows, columns] = low_ref[
                aligned(source * block_rows, block_rows, block_rows), :
            ]

    places = {}
    for units, (own_ref, send_ref) in zip(sets, outs):
        for unit in units:
            places[unit] = (own_ref, send_ref, columns_before(units, unit) // HEAD_SIZE)
    for head in range(0, heads, PACK):
        packed = range(head, min(head + PACK, heads))
        columns = [slice(h * HEAD_SIZE, (h + 1) * HEAD_SIZE) for h in packed]
        query_pieces, dscores, weights_low = heads_gradients(
            q_ref, g_ref, k_ref, v_ref, bias_ref, columns, block_count, block_rows
        )
        stacked = lambda ref, block: [ref[b * block_rows : (b + 1) * block_rows, c] for b in range(block, block_count) for c in columns]
        for block in range(block_count):
            seen = slice(block * block_rows, (block + 1) * block_rows)
            joined = lambda pieces: jnp.concatenate([p[seen, :] for p in pieces[block:]], axis=1)
            value_acc[seen, :] += contract(joined(weights_low), jnp.concatenate(stacked(g_ref, block), axis=0), (1, 0))
            key_acc[seen, :] += contract(joined(dscores), jnp.concatenate(stacked(q_ref, block), axis=0), (1, 0))
        for index, h in enumerate(packed):
            for block in range(block_count):
                low_ref[block * block_rows : (block + 1) * block_rows, :] = query_pieces[block][
                    index * block_rows : (index + 1) * block_rows, :
                ]
            put(*places[h])
    for unit, (own_ref, send_ref, at) in places.items():
        if unit < 0:
            key_sum, value_sum = sums[group_of(unit)]
            low_ref[...] = (key_sum[...] * HEAD_SIZE ** (-0.5)).astype(jnp.bfloat16)
            put(own_ref, send_ref, at)
            low_ref[...] = value_sum[...].astype(jnp.bfloat16)
            put(own_ref, send_ref, at + 1)
    if keeps:
        key_out[...] = key_acc[...]
        value_out[...] = value_acc[...]


def keys_and_values(group):
    return -1 - group


def group_of(unit):
    return -1 - unit


def columns_before(units, unit=None):
    ahead = units if unit is None else units[: units.index(unit)]
    return sum(HEAD_SIZE if u >= 0 else 2 * HEAD_SIZE for u in ahead)


def grads_chunk(
    starts, mapping, queries, gradient, keys, values, after, carried, start_head, heads, group, sets,
    vmem=FULL_VMEM,
):
    rows = queries.shape[0]
    block_count = starts.shape[0]
    block_rows = rows // block_count
    sent_groups = [group_of(u) for units in sets for u in units if u < 0]
    held = [g for g in carried if g == group or g in sent_groups]
    keeps = group not in sent_groups
    whole = lambda r, c: pl.BlockSpec((r, c), lambda i: (0, 0))
    cut = pl.BlockSpec((pl.Element(rows), pl.Element(heads * HEAD_SIZE)), lambda i: (0, start_head * HEAD_SIZE))
    group_spec = pl.BlockSpec((rows, HEAD_SIZE), lambda i: (0, group))
    running = jax.ShapeDtypeStruct((rows, HEAD_SIZE), jnp.float32)
    out_shape = []
    for units in sets:
        out_shape.append(jax.ShapeDtypeStruct((rows, columns_before(units)), jnp.bfloat16))
        out_shape.append(jax.ShapeDtypeStruct((CAP * block_rows, columns_before(units)), jnp.bfloat16))
    if keeps:
        out_shape += [running, running]
    out = pl.pallas_call(
        functools.partial(grads_kernel, block_count, block_rows, group, group not in held, keeps, held, heads, sets),
        grid=(1,),
        in_specs=[IN_SMEM] * 2
        + [cut, cut, group_spec, group_spec, ANYWHERE]
        + [whole(rows, HEAD_SIZE)] * (2 * len(held)),
        out_specs=[whole(*s.shape) for s in out_shape],
        out_shape=out_shape,
        scratch_shapes=[
            pltpu.VMEM((rows, rows), jnp.float32),
            pltpu.VMEM((rows, HEAD_SIZE), jnp.bfloat16),
            pltpu.VMEM((rows, HEAD_SIZE), jnp.float32),
            pltpu.VMEM((rows, HEAD_SIZE), jnp.float32),
        ],
        compiler_params=pltpu.CompilerParams(vmem_limit_bytes=vmem),
        cost_estimate=NO_COST,
    )(starts, mapping, queries, gradient, keys, values, after, *(x for g in held for x in carried[g]))
    carried = {g: sums for g, sums in carried.items() if g not in held}
    if keeps:
        carried[group] = tuple(out[2 * len(sets) :])
    return pairs_of(out[: 2 * len(sets)]), carried


def sort_kernel(block_count, block_rows, half_axis, peers, position_ref, mapping_ref, own_ref, arrived_ref, *refs):
    outs = refs[-peers:]
    at, peer = position_ref[0], position_ref[1]
    partner = lax.rem(at + half_axis, 2 * half_axis)
    arrived_slot = [jnp.int32(-1)] * block_count
    for index, block in enumerate(moved_blocks(mapping_ref, partner, block_count)):
        target = mapping_ref[partner * block_count + block] - at * block_count
        for slot in range(block_count):
            arrived_slot[slot] = jnp.where(target == slot, index, arrived_slot[slot])
    share = block_count * block_rows // peers
    step = math.gcd(share, block_rows)
    for hop, out_ref in enumerate(outs):
        to_peer = jnp.bitwise_xor(peer, hop)
        for piece in range(share // step):
            row = to_peer * share + piece * step
            block = lax.div(row, block_rows)
            slot = jnp.int32(-1)
            for b in range(block_count):
                slot = jnp.where(block == b, arrived_slot[b], slot)
            from_own = own_ref[aligned(row, step, step), :]
            from_pair = arrived_ref[
                aligned(jnp.maximum(slot, 0) * block_rows + lax.rem(row, block_rows), step, step), :
            ]
            out_ref[piece * step : (piece + 1) * step, :] = jnp.where(slot >= 0, from_pair, from_own)


def sort_rows(position, mapping, own, arrived, after, block_count, half_axis, peers):
    rows, columns = own.shape
    out = jax.ShapeDtypeStruct((rows // peers, columns), own.dtype)
    return pl.pallas_call(
        functools.partial(sort_kernel, block_count, rows // block_count, half_axis, peers),
        in_specs=[IN_SMEM, IN_SMEM, IN_VMEM, IN_VMEM] + [ANYWHERE] * len(after),
        out_specs=[IN_VMEM] * peers,
        out_shape=[out] * peers,
        compiler_params=pltpu.CompilerParams(vmem_limit_bytes=LITTLE_VMEM),
        cost_estimate=NO_COST,
    )(position, mapping, own, arrived, *after)


def place_kernel(peers, columns_here, places, held, position_ref, *refs):
    pieces = refs[: peers * len(places)]
    outs, sem = refs[-len(columns_here) - 1 : -1], refs[-1]
    peer = position_ref[1]
    copies = []
    for index, parts in enumerate(places):
        for hop in range(peers):
            from_peer = jnp.bitwise_xor(peer, hop)
            piece = pieces[index * peers + hop]
            for at, size, out, column in parts:
                copies.append(
                    pltpu.make_async_copy(
                        piece.at[:, at : at + size],
                        outs[out].at[:, aligned(from_peer * columns_here[out] + column, size, HEAD_SIZE)],
                        sem.at[len(copies)],
                    )
                )
                copies[-1].start()
    for copy in copies:
        copy.wait()


def joined_parts(parts):
    joined = []
    for at, size, out, column in parts:
        if joined and joined[-1][2] == out and joined[-1][0] + joined[-1][1] == at and joined[-1][3] + joined[-1][1] == column:
            joined[-1] = (joined[-1][0], joined[-1][1] + size, out, joined[-1][3])
        else:
            joined.append((at, size, out, column))
    return joined


def place_columns(position, pieces, places, columns_here, held, peers):
    rows = pieces[0][0].shape[0]
    flat = [p for chunk in pieces for p in chunk]
    count = peers * sum(len(parts) for parts in places)
    out_shape = [jax.ShapeDtypeStruct((rows, peers * c), pieces[0][0].dtype) for c in columns_here]
    return pl.pallas_call(
        functools.partial(place_kernel, peers, columns_here, places, len(held)),
        in_specs=[IN_SMEM] + [IN_VMEM] * len(flat) + [ANYWHERE] * len(held),
        out_specs=[ANYWHERE] * len(out_shape),
        out_shape=out_shape,
        input_output_aliases={1 + len(flat) + i: i for i in range(len(held))},
        scratch_shapes=[pltpu.SemaphoreType.DMA((count,))],
        compiler_params=pltpu.CompilerParams(vmem_limit_bytes=LITTLE_VMEM),
        cost_estimate=NO_COST,
    )(position, *flat, *held)


def plan_of(groups, repeats):
    lead = max(1, repeats // 2)
    heads = list(range(repeats))
    kernels = [(0, 0, lead, [heads[:lead]]), (0, lead, repeats - lead, [heads[: repeats - lead]])]
    for group in range(1, groups):
        kernels.append((group, 0, repeats, [heads[:lead], heads[lead:]]))
    for group in range(groups):
        kernels[-1][3].append([keys_and_values(group)])
    return kernels


def on_device(queries, key_layout_rows, value_layout_rows, output_gradient, doc_starts, block_mapping):
    rows = queries.shape[0]
    block_count = doc_starts.shape[0]
    groups = key_layout_rows.shape[1] // HEAD_SIZE
    repeats = queries.shape[1] // key_layout_rows.shape[1]
    axis_length = lax.axis_size("ctx")
    half_axis = axis_length // 2
    peers = lax.axis_size("tensor")
    position = jnp.stack([lax.axis_index("ctx"), lax.axis_index("tensor")]).astype(jnp.int32)
    pairs = [(i, (i + half_axis) % axis_length) for i in range(axis_length)]

    carried, after, sent = {}, key_layout_rows, []
    for number, (group, start, heads, sets) in enumerate(plan_of(groups, repeats)):
        made, carried = grads_chunk(
            doc_starts, block_mapping, queries, output_gradient, key_layout_rows, value_layout_rows,
            after, carried, group * repeats + start, heads, group, sets, FULL_VMEM if number == 0 else SOME_VMEM,
        )
        after = made[0][0]
        for units, (own, send) in zip(sets, made):
            sent.append((group * repeats + start, units, own, lax.ppermute(send, "ctx", pairs)))

    order, pieces, places = [after], [], []
    for start, units, own, arrived in sent:
        parts = sort_rows(position, block_mapping, own, arrived, order, block_count, half_axis, peers)
        got = [parts[0]] + [
            lax.ppermute(parts[hop], "tensor", [(i, i ^ hop) for i in range(peers)]) for hop in range(1, peers)
        ]
        order = [got[0]] + (list(pieces[-1][1:]) if pieces else [])
        pieces.append(got)
        parts = []
        for unit in units:
            at = columns_before(units, unit)
            if unit >= 0:
                parts.append((at, HEAD_SIZE, 0, (start + unit) * HEAD_SIZE))
            else:
                parts.append((at, HEAD_SIZE, 1, group_of(unit) * HEAD_SIZE))
                parts.append((at + HEAD_SIZE, HEAD_SIZE, 2, group_of(unit) * HEAD_SIZE))
        places.append(joined_parts(parts))
    columns_here = [queries.shape[1], key_layout_rows.shape[1], value_layout_rows.shape[1]]
    held = []
    if len(pieces) > 1:
        held = place_columns(position, pieces[:-1], places[:-1], columns_here, [], peers)
    return tuple(place_columns(position, pieces[-1:], places[-1:], columns_here, held, peers))


def solution(mesh):
    return jax.shard_map(
        on_device,
        mesh=mesh,
        in_specs=(
            P("ctx", "tensor"),
            P("ctx", "tensor"),
            P("ctx", "tensor"),
            P("ctx", "tensor"),
            P("ctx"),
            P(),
        ),
        out_specs=(
            P(("ctx", "tensor"), None),
            P(("ctx", "tensor"), None),
            P(("ctx", "tensor"), None),
        ),
        check_vma=False,
    )
```

```python
import functools
import math

import jax
import jax.numpy as jnp
from jax import lax
from jax.experimental import pallas as pl
from jax.experimental.pallas import tpu as pltpu
from jax.sharding import PartitionSpec as P

HEAD_SIZE = 128
CAP = 2
HIDDEN = -1e30
AT_ONCE = ()
FULL_VMEM, SOME_VMEM, LITTLE_VMEM = (60 << 20, 30 << 20, 8 << 20)
PACK = 4
NO_COST = pl.CostEstimate(flops=1000, bytes_accessed=1000, transcendentals=0)
IN_SMEM = pl.BlockSpec(memory_space=pltpu.SMEM)
IN_VMEM = pl.BlockSpec(memory_space=pltpu.VMEM)
ANYWHERE = pl.BlockSpec(memory_space=pl.ANY)


def contract(a, b, dims):
    return lax.dot_general(a, b, ((dims[:1], dims[1:]), ((), ())), preferred_element_type=jnp.float32)


def aligned(start, size, step):
    return pl.ds(pl.multiple_of(start, step), size)


def own_sources(mapping_ref, position, block_count):
    sources = [jnp.int32(-1)] * block_count
    for block in range(block_count):
        target = mapping_ref[position * block_count + block] - position * block_count
        for slot in range(block_count):
            sources[slot] = jnp.where(target == slot, block, sources[slot])
    return sources


def moved_blocks(mapping_ref, position, block_count):
    moved = [jnp.int32(0)] * CAP
    seen = jnp.int32(0)
    for block in range(block_count):
        target = mapping_ref[position * block_count + block] - position * block_count
        leaves = (target < 0) | (target >= block_count)
        for slot in range(CAP):
            moved[slot] = jnp.where(leaves & (seen <= slot), block, moved[slot])
        seen = seen + jnp.where(leaves, 1, 0)
    return moved


def heads_gradients(q_ref, g_ref, k_ref, v_ref, bias_ref, columns, block_count, block_rows):
    rate = HEAD_SIZE ** (-0.5) * math.log2(math.e)
    weights_low, dscores, query_pieces = [], [], []
    for block in range(block_count):
        rows = slice(block * block_rows, (block + 1) * block_rows)
        width = (block + 1) * block_rows
        q = jnp.concatenate([q_ref[rows, c] for c in columns], axis=0)
        g = jnp.concatenate([g_ref[rows, c] for c in columns], axis=0)
        k, v = k_ref[:width, :], v_ref[:width, :]
        bias = jnp.concatenate([bias_ref[:width, rows]] * len(columns), axis=1)
        scores = contract(k, q, (1, 1)) + bias
        top = jnp.max(scores, axis=0, keepdims=True)
        weights = jnp.exp2((scores - top) * rate)
        dprobs = contract(v, g, (1, 1))
        share = 1.0 / jnp.sum(weights, axis=0, keepdims=True)
        delta = jnp.sum(weights * dprobs, axis=0, keepdims=True) * share
        weights = weights * share
        weights_low.append(weights.astype(jnp.bfloat16))
        dscores.append((weights * (dprobs - delta)).astype(jnp.bfloat16))
        query_pieces.append((contract(dscores[-1], k, (0, 0)) * HEAD_SIZE ** (-0.5)).astype(jnp.bfloat16))
    return query_pieces, dscores, weights_low


def pairs_of(refs):
    return list(zip(refs[::2], refs[1::2]))


def grads_kernel(block_count, block_rows, group, first, keeps, held, heads, sets, *refs):
    starts_ref, mapping_ref, q_ref, g_ref, k_ref, v_ref, _, *refs = refs
    sums, refs = dict(zip(held, pairs_of(refs[: 2 * len(held)]))), refs[2 * len(held) :]
    outs, refs = pairs_of(refs[: 2 * len(sets)]), refs[2 * len(sets) :]
    if keeps:
        key_out, value_out, *refs = refs
    bias_ref, low_ref, key_acc, value_acc = refs
    position = lax.axis_index("ctx")
    rows = block_count * block_rows

    document_row = jnp.int32(0)
    for block in range(block_count):
        document_row = jnp.where(starts_ref[block] != 0, block * block_rows, document_row)
        width = (block + 1) * block_rows
        at_key = lax.broadcasted_iota(jnp.int32, (width, block_rows), 0)
        at_row = lax.broadcasted_iota(jnp.int32, (width, block_rows), 1) + block * block_rows
        visible = (at_key <= at_row) & (at_key >= document_row)
        bias_ref[:width, block * block_rows : width] = jnp.where(visible, 0.0, HIDDEN)
    if first:
        key_acc[...] = jnp.zeros_like(key_acc)
        value_acc[...] = jnp.zeros_like(value_acc)
    else:
        key_acc[...] = sums[group][0][...]
        value_acc[...] = sums[group][1][...]
    sums[group] = (key_acc, value_acc)

    owned = [jnp.maximum(source, 0) for source in own_sources(mapping_ref, position, block_count)]
    moved = moved_blocks(mapping_ref, position, block_count)

    def put(own_ref, send_ref, at):
        columns = slice(at * HEAD_SIZE, (at + 1) * HEAD_SIZE)
        for slot, source in enumerate(owned):
            own_ref[slot * block_rows : (slot + 1) * block_rows, columns] = low_ref[
                aligned(source * block_rows, block_rows, block_rows), :
            ]
        for slot, source in enumerate(moved):
            send_ref[slot * block_rows : (slot + 1) * block_rows, columns] = low_ref[
                aligned(source * block_rows, block_rows, block_rows), :
            ]

    places = {}
    for units, (own_ref, send_ref) in zip(sets, outs):
        for unit in units:
            places[unit] = (own_ref, send_ref, columns_before(units, unit) // HEAD_SIZE)
    for head in range(0, heads, PACK):
        packed = range(head, min(head + PACK, heads))
        columns = [slice(h * HEAD_SIZE, (h + 1) * HEAD_SIZE) for h in packed]
        query_pieces, dscores, weights_low = heads_gradients(
            q_ref, g_ref, k_ref, v_ref, bias_ref, columns, block_count, block_rows
        )
        stacked = lambda ref, block: [ref[b * block_rows : (b + 1) * block_rows, c] for b in range(block, block_count) for c in columns]
        for block in range(block_count):
            seen = slice(block * block_rows, (block + 1) * block_rows)
            joined = lambda pieces: jnp.concatenate([p[seen, :] for p in pieces[block:]], axis=1)
            value_acc[seen, :] += contract(joined(weights_low), jnp.concatenate(stacked(g_ref, block), axis=0), (1, 0))
            key_acc[seen, :] += contract(joined(dscores), jnp.concatenate(stacked(q_ref, block), axis=0), (1, 0))
        for index, h in enumerate(packed):
            for block in range(block_count):
                low_ref[block * block_rows : (block + 1) * block_rows, :] = query_pieces[block][
                    index * block_rows : (index + 1) * block_rows, :
                ]
            put(*places[h])
    for unit, (own_ref, send_ref, at) in places.items():
        if unit < 0:
            key_sum, value_sum = sums[group_of(unit)]
            low_ref[...] = (key_sum[...] * HEAD_SIZE ** (-0.5)).astype(jnp.bfloat16)
            put(own_ref, send_ref, at)
            low_ref[...] = value_sum[...].astype(jnp.bfloat16)
            put(own_ref, send_ref, at + 1)
    if keeps:
        key_out[...] = key_acc[...]
        value_out[...] = value_acc[...]


def keys_and_values(group):
    return -1 - group


def group_of(unit):
    return -1 - unit


def columns_before(units, unit=None):
    ahead = units if unit is None else units[: units.index(unit)]
    return sum(HEAD_SIZE if u >= 0 else 2 * HEAD_SIZE for u in ahead)


def grads_chunk(
    starts, mapping, queries, gradient, keys, values, after, carried, start_head, heads, group, sets,
    vmem=FULL_VMEM,
):
    rows = queries.shape[0]
    block_count = starts.shape[0]
    block_rows = rows // block_count
    sent_groups = [group_of(u) for units in sets for u in units if u < 0]
    held = [g for g in carried if g == group or g in sent_groups]
    keeps = group not in sent_groups
    whole = lambda r, c: pl.BlockSpec((r, c), lambda i: (0, 0))
    cut = pl.BlockSpec((pl.Element(rows), pl.Element(heads * HEAD_SIZE)), lambda i: (0, start_head * HEAD_SIZE))
    group_spec = pl.BlockSpec((rows, HEAD_SIZE), lambda i: (0, group))
    running = jax.ShapeDtypeStruct((rows, HEAD_SIZE), jnp.float32)
    out_shape = []
    for units in sets:
        out_shape.append(jax.ShapeDtypeStruct((rows, columns_before(units)), jnp.bfloat16))
        out_shape.append(jax.ShapeDtypeStruct((CAP * block_rows, columns_before(units)), jnp.bfloat16))
    if keeps:
        out_shape += [running, running]
    out = pl.pallas_call(
        functools.partial(grads_kernel, block_count, block_rows, group, group not in held, keeps, held, heads, sets),
        grid=(1,),
        in_specs=[IN_SMEM] * 2
        + [cut, cut, group_spec, group_spec, ANYWHERE]
        + [whole(rows, HEAD_SIZE)] * (2 * len(held)),
        out_specs=[whole(*s.shape) for s in out_shape],
        out_shape=out_shape,
        scratch_shapes=[
            pltpu.VMEM((rows, rows), jnp.float32),
            pltpu.VMEM((rows, HEAD_SIZE), jnp.bfloat16),
            pltpu.VMEM((rows, HEAD_SIZE), jnp.float32),
            pltpu.VMEM((rows, HEAD_SIZE), jnp.float32),
        ],
        compiler_params=pltpu.CompilerParams(vmem_limit_bytes=vmem),
        cost_estimate=NO_COST,
    )(starts, mapping, queries, gradient, keys, values, after, *(x for g in held for x in carried[g]))
    carried = {g: sums for g, sums in carried.items() if g not in held}
    if keeps:
        carried[group] = tuple(out[2 * len(sets) :])
    return pairs_of(out[: 2 * len(sets)]), carried


def sort_kernel(block_count, block_rows, half_axis, peers, in_order, position_ref, mapping_ref, own_ref, arrived_ref, *refs):
    outs = [refs[-1].at[p] for p in range(peers)] if in_order else refs[-peers:]
    at, peer = position_ref[0], position_ref[1]
    partner = lax.rem(at + half_axis, 2 * half_axis)
    arrived_slot = [jnp.int32(-1)] * block_count
    for index, block in enumerate(moved_blocks(mapping_ref, partner, block_count)):
        target = mapping_ref[partner * block_count + block] - at * block_count
        for slot in range(block_count):
            arrived_slot[slot] = jnp.where(target == slot, index, arrived_slot[slot])
    share = block_count * block_rows // peers
    step = math.gcd(share, block_rows)
    for hop, out_ref in enumerate(outs):
        to_peer = hop if in_order else jnp.bitwise_xor(peer, hop)
        for piece in range(share // step):
            row = to_peer * share + piece * step
            block = lax.div(jnp.int32(row), jnp.int32(block_rows))
            slot = jnp.int32(-1)
            for b in range(block_count):
                slot = jnp.where(block == b, arrived_slot[b], slot)
            from_own = own_ref[aligned(row, step, step), :]
            from_pair = arrived_ref[
                aligned(jnp.maximum(slot, 0) * block_rows + lax.rem(jnp.int32(row), jnp.int32(block_rows)), step, step), :
            ]
            out_ref[piece * step : (piece + 1) * step, :] = jnp.where(slot >= 0, from_pair, from_own)


def sort_rows(position, mapping, own, arrived, after, block_count, half_axis, peers, in_order):
    rows, columns = own.shape
    if in_order:
        out = [jax.ShapeDtypeStruct((peers, rows // peers, columns), own.dtype)]
    else:
        out = [jax.ShapeDtypeStruct((rows // peers, columns), own.dtype)] * peers
    return pl.pallas_call(
        functools.partial(sort_kernel, block_count, rows // block_count, half_axis, peers, in_order),
        in_specs=[IN_SMEM, IN_SMEM, IN_VMEM, IN_VMEM] + [ANYWHERE] * len(after),
        out_specs=[IN_VMEM] * len(out),
        out_shape=out,
        compiler_params=pltpu.CompilerParams(vmem_limit_bytes=LITTLE_VMEM),
        cost_estimate=NO_COST,
    )(position, mapping, own, arrived, *after)


def place_kernel(peers, columns_here, places, held, position_ref, *refs):
    pieces = list(refs)
    outs, sem = refs[-len(columns_here) - 1 : -1], refs[-1]
    peer = position_ref[1]
    copies = []
    for in_order, parts in places:
        chunk = pieces.pop(0) if in_order else None
        for hop in range(peers):
            from_peer = hop if in_order else jnp.bitwise_xor(peer, hop)
            piece = chunk.at[hop] if in_order else pieces.pop(0)
            for at, size, out, column in parts:
                copies.append(
                    pltpu.make_async_copy(
                        piece.at[:, at : at + size],
                        outs[out].at[:, aligned(from_peer * columns_here[out] + column, size, HEAD_SIZE)],
                        sem.at[len(copies)],
                    )
                )
                copies[-1].start()
    for copy in copies:
        copy.wait()


def spread_kernel(block_count, block_rows, half_axis, peers, position_ref, mapping_ref, own_ref, send_ref, out_ref):
    at = position_ref[0]
    partner = lax.rem(at + half_axis, 2 * half_axis)
    send_slot = [jnp.int32(0)] * block_count
    for index, block in enumerate(moved_blocks(mapping_ref, at, block_count)):
        target = mapping_ref[at * block_count + block] - partner * block_count
        for slot in range(block_count):
            send_slot[slot] = jnp.where(target == slot, index, send_slot[slot])
    share = block_count * block_rows // peers
    step = math.gcd(share, block_rows)
    for peer in range(peers):
        out_ref[peer, 0] = own_ref[peer * share : (peer + 1) * share, :]
        for piece in range(share // step):
            row = peer * share + piece * step
            at_send = send_slot[row // block_rows] * block_rows + row % block_rows
            out_ref[peer, 1, piece * step : (piece + 1) * step, :] = send_ref[aligned(at_send, step, step), :]


def spread_rows(position, mapping, own, send, half_axis, block_count, peers):
    rows, columns = own.shape
    return pl.pallas_call(
        functools.partial(spread_kernel, block_count, rows // block_count, half_axis, peers),
        in_specs=[IN_SMEM, IN_SMEM, IN_VMEM, IN_VMEM],
        out_specs=IN_VMEM,
        out_shape=jax.ShapeDtypeStruct((peers, 2, rows // peers, columns), own.dtype),
        compiler_params=pltpu.CompilerParams(vmem_limit_bytes=LITTLE_VMEM),
        cost_estimate=NO_COST,
    )(position, mapping, own, send)


def place_last_kernel(block_count, block_rows, peers, columns_here, parts, *refs):
    position_ref, mapping_ref, spread_ref, arrived_ref, *refs = refs
    outs, merged_ref, sem = refs[-len(columns_here) - 2 : -2], refs[-2], refs[-1]
    here = own_sources(mapping_ref, position_ref[0], block_count)
    share = block_count * block_rows // peers
    step = math.gcd(share, block_rows)
    for piece in range(share // step):
        block = lax.div(position_ref[1] * share + piece * step, block_rows)
        source = jnp.int32(-1)
        for slot in range(block_count):
            source = jnp.where(block == slot, here[slot], source)
        rows = slice(piece * step, (piece + 1) * step)
        for peer in range(peers):
            merged_ref[peer, rows, :] = jnp.where(source >= 0, spread_ref[peer, 0, rows, :], arrived_ref[peer, rows, :])
    copies = []
    for peer in range(peers):
        for at, size, out, column in parts:
            start = peer * columns_here[out] + column
            copies.append(
                pltpu.make_async_copy(
                    merged_ref.at[peer, :, at : at + size], outs[out].at[:, start : start + size], sem.at[len(copies)]
                )
            )
            copies[-1].start()
    for copy in copies:
        copy.wait()


def place_last(position, mapping, spread, arrived, parts, columns_here, held, block_count):
    peers, _, share, columns = spread.shape
    return pl.pallas_call(
        functools.partial(
            place_last_kernel, block_count, share * peers // block_count, peers, columns_here, parts
        ),
        in_specs=[IN_SMEM, IN_SMEM, IN_VMEM, IN_VMEM] + [ANYWHERE] * len(held),
        out_specs=[ANYWHERE] * len(held),
        out_shape=[jax.ShapeDtypeStruct(h.shape, h.dtype) for h in held],
        input_output_aliases={4 + i: i for i in range(len(held))},
        scratch_shapes=[
            pltpu.VMEM((peers, share, columns), spread.dtype),
            pltpu.SemaphoreType.DMA((peers * len(parts),)),
        ],
        compiler_params=pltpu.CompilerParams(vmem_limit_bytes=LITTLE_VMEM),
        cost_estimate=NO_COST,
    )(position, mapping, spread, arrived, *held)


def joined_parts(parts):
    joined = []
    for at, size, out, column in parts:
        if joined and joined[-1][2] == out and joined[-1][0] + joined[-1][1] == at and joined[-1][3] + joined[-1][1] == column:
            joined[-1] = (joined[-1][0], joined[-1][1] + size, out, joined[-1][3])
        else:
            joined.append((at, size, out, column))
    return joined


def place_columns(position, pieces, places, columns_here, held, peers):
    rows, dtype = pieces[0][0].shape[-2], pieces[0][0].dtype
    flat = [p for chunk in pieces for p in chunk]
    count = peers * sum(len(parts) for _, parts in places)
    out_shape = [jax.ShapeDtypeStruct((rows, peers * c), dtype) for c in columns_here]
    return pl.pallas_call(
        functools.partial(place_kernel, peers, columns_here, places, len(held)),
        in_specs=[IN_SMEM] + [IN_VMEM] * len(flat) + [ANYWHERE] * len(held),
        out_specs=[ANYWHERE] * len(out_shape),
        out_shape=out_shape,
        input_output_aliases={1 + len(flat) + i: i for i in range(len(held))},
        scratch_shapes=[pltpu.SemaphoreType.DMA((count,))],
        compiler_params=pltpu.CompilerParams(vmem_limit_bytes=LITTLE_VMEM),
        cost_estimate=NO_COST,
    )(position, *flat, *held)


def plan_of(groups, repeats):
    lead, cut = max(1, 5 * repeats // 8), max(1, 4 * repeats // 8)
    heads = list(range(repeats))
    kernels = [(0, 0, lead, [heads[:lead]]), (0, lead, repeats - lead, [heads[: repeats - lead]])]
    for group in range(1, groups):
        kernels.append((group, 0, repeats, [heads[:cut], heads[cut:]]))
    for group in range(groups - 1):
        kernels[group + 1][3][-1].append(keys_and_values(group))
    kernels[-1][3].append([keys_and_values(groups - 1)])
    return kernels


def on_device(queries, key_layout_rows, value_layout_rows, output_gradient, doc_starts, block_mapping):
    rows = queries.shape[0]
    block_count = doc_starts.shape[0]
    groups = key_layout_rows.shape[1] // HEAD_SIZE
    repeats = queries.shape[1] // key_layout_rows.shape[1]
    axis_length = lax.axis_size("ctx")
    half_axis = axis_length // 2
    peers = lax.axis_size("tensor")
    position = jnp.stack([lax.axis_index("ctx"), lax.axis_index("tensor")]).astype(jnp.int32)
    pairs = [(i, (i + half_axis) % axis_length) for i in range(axis_length)]

    carried, after, sent = {}, key_layout_rows, []
    for number, (group, start, heads, sets) in enumerate(plan_of(groups, repeats)):
        made, carried = grads_chunk(
            doc_starts, block_mapping, queries, output_gradient, key_layout_rows, value_layout_rows,
            after, carried, group * repeats + start, heads, group, sets, FULL_VMEM if number == 0 else SOME_VMEM,
        )
        after = made[0][0]
        for units, (own, send) in zip(sets, made):
            sent.append((group * repeats + start, units, own, send))

    *sent, (_, last_units, own, send) = sent
    sent = [(start, units, own, lax.ppermute(send, "ctx", pairs)) for start, units, own, send in sent]
    spread = spread_rows(position, block_mapping, own, send, half_axis, block_count, peers)
    spread = lax.all_to_all(spread, "tensor", split_axis=0, concat_axis=0, tiled=True)
    last_arrived = lax.ppermute(spread[:, 1], "ctx", pairs)

    def parts_of(start, units):
        parts = []
        for unit in units:
            at = columns_before(units, unit)
            if unit >= 0:
                parts.append((at, HEAD_SIZE, 0, (start + unit) * HEAD_SIZE))
            else:
                parts.append((at, HEAD_SIZE, 1, group_of(unit) * HEAD_SIZE))
                parts.append((at + HEAD_SIZE, HEAD_SIZE, 2, group_of(unit) * HEAD_SIZE))
        return joined_parts(parts)

    order, pieces, places = [after], [], []
    for index, (start, units, own, arrived) in enumerate(sent):
        at_once = index in AT_ONCE
        got = sort_rows(position, block_mapping, own, arrived, order, block_count, half_axis, peers, at_once)
        if at_once:
            got = [lax.all_to_all(got[0], "tensor", split_axis=0, concat_axis=0, tiled=True)]
        else:
            got = [got[0]] + [
                lax.ppermute(got[hop], "tensor", [(i, i ^ hop) for i in range(peers)]) for hop in range(1, peers)
            ]
        order = [got[0], got[1]] + (list(pieces[-1][2:]) if pieces else [])
        pieces.append(got)
        places.append((at_once, parts_of(start, units)))
    columns_here = [queries.shape[1], key_layout_rows.shape[1], value_layout_rows.shape[1]]
    held = place_columns(position, pieces, places, columns_here, [], peers)
    parts = parts_of(0, last_units)
    return tuple(
        place_last(position, block_mapping, spread, last_arrived, parts, columns_here, held, block_count)
    )


def solution(mesh):
    return jax.shard_map(
        on_device,
        mesh=mesh,
        in_specs=(
            P("ctx", "tensor"),
            P("ctx", "tensor"),
            P("ctx", "tensor"),
            P("ctx", "tensor"),
            P("ctx"),
            P(),
        ),
        out_specs=(
            P(("ctx", "tensor"), None),
            P(("ctx", "tensor"), None),
            P(("ctx", "tensor"), None),
        ),
        check_vma=False,
    )
```

```python
import functools
import math

import jax
import jax.numpy as jnp
from jax import lax
from jax.experimental import pallas as pl
from jax.experimental.pallas import tpu as pltpu
from jax.sharding import PartitionSpec as P

HEAD_SIZE = 128
CAP = 2
HIDDEN = -1e30
FULL_VMEM, SOME_VMEM, LITTLE_VMEM = (60 << 20, 30 << 20, 8 << 20)
PACK = 4
NO_COST = pl.CostEstimate(flops=1000, bytes_accessed=1000, transcendentals=0)
IN_SMEM = pl.BlockSpec(memory_space=pltpu.SMEM)
IN_VMEM = pl.BlockSpec(memory_space=pltpu.VMEM)
ANYWHERE = pl.BlockSpec(memory_space=pl.ANY)


def contract(a, b, dims):
    return lax.dot_general(a, b, ((dims[:1], dims[1:]), ((), ())), preferred_element_type=jnp.float32)


def aligned(start, size, step):
    return pl.ds(pl.multiple_of(start, step), size)


def own_sources(mapping_ref, position, block_count):
    sources = [jnp.int32(-1)] * block_count
    for block in range(block_count):
        target = mapping_ref[position * block_count + block] - position * block_count
        for slot in range(block_count):
            sources[slot] = jnp.where(target == slot, block, sources[slot])
    return sources


def moved_blocks(mapping_ref, position, block_count):
    moved = [jnp.int32(0)] * CAP
    seen = jnp.int32(0)
    for block in range(block_count):
        target = mapping_ref[position * block_count + block] - position * block_count
        leaves = (target < 0) | (target >= block_count)
        for slot in range(CAP):
            moved[slot] = jnp.where(leaves & (seen <= slot), block, moved[slot])
        seen = seen + jnp.where(leaves, 1, 0)
    return moved


def heads_gradients(q_ref, g_ref, k_ref, v_ref, bias_ref, columns, block_count, block_rows):
    rate = HEAD_SIZE ** (-0.5) * math.log2(math.e)
    weights_low, dscores, query_pieces = [], [], []
    for block in range(block_count):
        rows = slice(block * block_rows, (block + 1) * block_rows)
        width = (block + 1) * block_rows
        q = jnp.concatenate([q_ref[rows, c] for c in columns], axis=0)
        g = jnp.concatenate([g_ref[rows, c] for c in columns], axis=0)
        k, v = k_ref[:width, :], v_ref[:width, :]
        bias = jnp.concatenate([bias_ref[:width, rows]] * len(columns), axis=1)
        scores = contract(k, q, (1, 1)) + bias
        top = jnp.max(scores, axis=0, keepdims=True)
        weights = jnp.exp2((scores - top) * rate)
        dprobs = contract(v, g, (1, 1))
        share = 1.0 / jnp.sum(weights, axis=0, keepdims=True)
        delta = jnp.sum(weights * dprobs, axis=0, keepdims=True) * share
        weights = weights * share
        weights_low.append(weights.astype(jnp.bfloat16))
        dscores.append((weights * (dprobs - delta)).astype(jnp.bfloat16))
        query_pieces.append((contract(dscores[-1], k, (0, 0)) * HEAD_SIZE ** (-0.5)).astype(jnp.bfloat16))
    return query_pieces, dscores, weights_low


def pairs_of(refs):
    return list(zip(refs[::2], refs[1::2]))


def grads_kernel(block_count, block_rows, group, first, keeps, held, heads, sets, *refs):
    starts_ref, mapping_ref, q_ref, g_ref, k_ref, v_ref, _, *refs = refs
    sums, refs = dict(zip(held, pairs_of(refs[: 2 * len(held)]))), refs[2 * len(held) :]
    outs, refs = pairs_of(refs[: 2 * len(sets)]), refs[2 * len(sets) :]
    if keeps:
        key_out, value_out, *refs = refs
    bias_ref, low_ref, key_acc, value_acc = refs
    position = lax.axis_index("ctx")
    rows = block_count * block_rows

    document_row = jnp.int32(0)
    for block in range(block_count):
        document_row = jnp.where(starts_ref[block] != 0, block * block_rows, document_row)
        width = (block + 1) * block_rows
        at_key = lax.broadcasted_iota(jnp.int32, (width, block_rows), 0)
        at_row = lax.broadcasted_iota(jnp.int32, (width, block_rows), 1) + block * block_rows
        visible = (at_key <= at_row) & (at_key >= document_row)
        bias_ref[:width, block * block_rows : width] = jnp.where(visible, 0.0, HIDDEN)
    if first:
        key_acc[...] = jnp.zeros_like(key_acc)
        value_acc[...] = jnp.zeros_like(value_acc)
    else:
        key_acc[...] = sums[group][0][...]
        value_acc[...] = sums[group][1][...]
    sums[group] = (key_acc, value_acc)

    owned = [jnp.maximum(source, 0) for source in own_sources(mapping_ref, position, block_count)]
    moved = moved_blocks(mapping_ref, position, block_count)

    def put(own_ref, send_ref, at):
        columns = slice(at * HEAD_SIZE, (at + 1) * HEAD_SIZE)
        for slot, source in enumerate(owned):
            own_ref[slot * block_rows : (slot + 1) * block_rows, columns] = low_ref[
                aligned(source * block_rows, block_rows, block_rows), :
            ]
        for slot, source in enumerate(moved):
            send_ref[slot * block_rows : (slot + 1) * block_rows, columns] = low_ref[
                aligned(source * block_rows, block_rows, block_rows), :
            ]

    places = {}
    for units, (own_ref, send_ref) in zip(sets, outs):
        for unit in units:
            places[unit] = (own_ref, send_ref, columns_before(units, unit) // HEAD_SIZE)
    for head in range(0, heads, PACK):
        packed = range(head, min(head + PACK, heads))
        columns = [slice(h * HEAD_SIZE, (h + 1) * HEAD_SIZE) for h in packed]
        query_pieces, dscores, weights_low = heads_gradients(
            q_ref, g_ref, k_ref, v_ref, bias_ref, columns, block_count, block_rows
        )
        stacked = lambda ref, block: [ref[b * block_rows : (b + 1) * block_rows, c] for b in range(block, block_count) for c in columns]
        for block in range(block_count):
            seen = slice(block * block_rows, (block + 1) * block_rows)
            joined = lambda pieces: jnp.concatenate([p[seen, :] for p in pieces[block:]], axis=1)
            value_acc[seen, :] += contract(joined(weights_low), jnp.concatenate(stacked(g_ref, block), axis=0), (1, 0))
            key_acc[seen, :] += contract(joined(dscores), jnp.concatenate(stacked(q_ref, block), axis=0), (1, 0))
        for index, h in enumerate(packed):
            for block in range(block_count):
                low_ref[block * block_rows : (block + 1) * block_rows, :] = query_pieces[block][
                    index * block_rows : (index + 1) * block_rows, :
                ]
            put(*places[h])
    for unit, (own_ref, send_ref, at) in places.items():
        if unit < 0:
            key_sum, value_sum = sums[group_of(unit)]
            low_ref[...] = (key_sum[...] * HEAD_SIZE ** (-0.5)).astype(jnp.bfloat16)
            put(own_ref, send_ref, at)
            low_ref[...] = value_sum[...].astype(jnp.bfloat16)
            put(own_ref, send_ref, at + 1)
    if keeps:
        key_out[...] = key_acc[...]
        value_out[...] = value_acc[...]


def keys_and_values(group):
    return -1 - group


def group_of(unit):
    return -1 - unit


def columns_before(units, unit=None):
    ahead = units if unit is None else units[: units.index(unit)]
    return sum(HEAD_SIZE if u >= 0 else 2 * HEAD_SIZE for u in ahead)


def grads_chunk(
    starts, mapping, queries, gradient, keys, values, after, carried, start_head, heads, group, sets,
    vmem=FULL_VMEM,
):
    rows = queries.shape[0]
    block_count = starts.shape[0]
    block_rows = rows // block_count
    sent_groups = [group_of(u) for units in sets for u in units if u < 0]
    held = [g for g in carried if g == group or g in sent_groups]
    keeps = group not in sent_groups
    whole = lambda r, c: pl.BlockSpec((r, c), lambda i: (0, 0))
    cut = pl.BlockSpec((pl.Element(rows), pl.Element(heads * HEAD_SIZE)), lambda i: (0, start_head * HEAD_SIZE))
    group_spec = pl.BlockSpec((rows, HEAD_SIZE), lambda i: (0, group))
    running = jax.ShapeDtypeStruct((rows, HEAD_SIZE), jnp.float32)
    out_shape = []
    for units in sets:
        out_shape.append(jax.ShapeDtypeStruct((rows, columns_before(units)), jnp.bfloat16))
        out_shape.append(jax.ShapeDtypeStruct((CAP * block_rows, columns_before(units)), jnp.bfloat16))
    if keeps:
        out_shape += [running, running]
    out = pl.pallas_call(
        functools.partial(grads_kernel, block_count, block_rows, group, group not in held, keeps, held, heads, sets),
        grid=(1,),
        in_specs=[IN_SMEM] * 2
        + [cut, cut, group_spec, group_spec, ANYWHERE]
        + [whole(rows, HEAD_SIZE)] * (2 * len(held)),
        out_specs=[whole(*s.shape) for s in out_shape],
        out_shape=out_shape,
        scratch_shapes=[
            pltpu.VMEM((rows, rows), jnp.float32),
            pltpu.VMEM((rows, HEAD_SIZE), jnp.bfloat16),
            pltpu.VMEM((rows, HEAD_SIZE), jnp.float32),
            pltpu.VMEM((rows, HEAD_SIZE), jnp.float32),
        ],
        compiler_params=pltpu.CompilerParams(vmem_limit_bytes=vmem),
        cost_estimate=NO_COST,
    )(starts, mapping, queries, gradient, keys, values, after, *(x for g in held for x in carried[g]))
    carried = {g: sums for g, sums in carried.items() if g not in held}
    if keeps:
        carried[group] = tuple(out[2 * len(sets) :])
    return pairs_of(out[: 2 * len(sets)]), carried


def sort_kernel(block_count, block_rows, half_axis, peers, widths, position_ref, mapping_ref, *refs):
    sources, outs = pairs_of(refs[: 2 * len(widths)]), refs[-peers:]
    at, peer = position_ref[0], position_ref[1]
    partner = lax.rem(at + half_axis, 2 * half_axis)
    arrived_slot = [jnp.int32(-1)] * block_count
    for index, block in enumerate(moved_blocks(mapping_ref, partner, block_count)):
        target = mapping_ref[partner * block_count + block] - at * block_count
        for slot in range(block_count):
            arrived_slot[slot] = jnp.where(target == slot, index, arrived_slot[slot])
    share = block_count * block_rows // peers
    step = math.gcd(share, block_rows)
    for hop, out_ref in enumerate(outs):
        to_peer = jnp.bitwise_xor(peer, hop)
        for piece in range(share // step):
            row = to_peer * share + piece * step
            block = lax.div(row, block_rows)
            slot = jnp.int32(-1)
            for b in range(block_count):
                slot = jnp.where(block == b, arrived_slot[b], slot)
            at_pair = jnp.maximum(slot, 0) * block_rows + lax.rem(row, block_rows)
            column = 0
            for (own_ref, arrived_ref), width in zip(sources, widths):
                from_own = own_ref[aligned(row, step, step), :]
                from_pair = arrived_ref[aligned(at_pair, step, step), :]
                out_ref[piece * step : (piece + 1) * step, column : column + width] = jnp.where(
                    slot >= 0, from_pair, from_own
                )
                column += width


def sort_rows(position, mapping, sources, after, block_count, half_axis, peers):
    rows = sources[0][0].shape[0]
    widths = [own.shape[1] for own, _ in sources]
    out = jax.ShapeDtypeStruct((rows // peers, sum(widths)), sources[0][0].dtype)
    return pl.pallas_call(
        functools.partial(sort_kernel, block_count, rows // block_count, half_axis, peers, widths),
        in_specs=[IN_SMEM, IN_SMEM] + [IN_VMEM] * (2 * len(sources)) + [ANYWHERE] * len(after),
        out_specs=[IN_VMEM] * peers,
        out_shape=[out] * peers,
        compiler_params=pltpu.CompilerParams(vmem_limit_bytes=LITTLE_VMEM),
        cost_estimate=NO_COST,
    )(position, mapping, *(x for source in sources for x in source), *after)


def place_kernel(peers, columns_here, places, held, position_ref, *refs):
    pieces = list(refs)
    outs, sem = refs[-len(columns_here) - 1 : -1], refs[-1]
    peer = position_ref[1]
    copies = []
    for parts in places:
        for hop in range(peers):
            from_peer = jnp.bitwise_xor(peer, hop)
            piece = pieces.pop(0)
            for at, size, out, column in parts:
                copies.append(
                    pltpu.make_async_copy(
                        piece.at[:, at : at + size],
                        outs[out].at[:, aligned(from_peer * columns_here[out] + column, size, HEAD_SIZE)],
                        sem.at[len(copies)],
                    )
                )
                copies[-1].start()
    for copy in copies:
        copy.wait()


def spread_kernel(block_count, block_rows, half_axis, peers, position_ref, mapping_ref, own_ref, send_ref, _, out_ref):
    at = position_ref[0]
    partner = lax.rem(at + half_axis, 2 * half_axis)
    send_slot = [jnp.int32(0)] * block_count
    for index, block in enumerate(moved_blocks(mapping_ref, at, block_count)):
        target = mapping_ref[at * block_count + block] - partner * block_count
        for slot in range(block_count):
            send_slot[slot] = jnp.where(target == slot, index, send_slot[slot])
    share = block_count * block_rows // peers
    step = math.gcd(share, block_rows)
    for peer in range(peers):
        out_ref[peer, 0] = own_ref[peer * share : (peer + 1) * share, :]
        for piece in range(share // step):
            row = peer * share + piece * step
            at_send = send_slot[row // block_rows] * block_rows + row % block_rows
            out_ref[peer, 1, piece * step : (piece + 1) * step, :] = send_ref[aligned(at_send, step, step), :]


def spread_rows(position, mapping, own, send, after, half_axis, block_count, peers):
    rows, columns = own.shape
    return pl.pallas_call(
        functools.partial(spread_kernel, block_count, rows // block_count, half_axis, peers),
        in_specs=[IN_SMEM, IN_SMEM, IN_VMEM, IN_VMEM, ANYWHERE],
        out_specs=IN_VMEM,
        out_shape=jax.ShapeDtypeStruct((peers, 2, rows // peers, columns), own.dtype),
        compiler_params=pltpu.CompilerParams(vmem_limit_bytes=LITTLE_VMEM),
        cost_estimate=NO_COST,
    )(position, mapping, own, send, after)


def place_last_kernel(block_count, block_rows, peers, columns_here, parts, piece_parts, *refs):
    position_ref, mapping_ref, spread_ref, arrived_ref, *refs = refs
    pieces = refs[:peers]
    outs, merged_ref, sem = refs[-len(columns_here) - 2 : -2], refs[-2], refs[-1]
    copies = []
    for hop, piece in enumerate(pieces):
        from_peer = jnp.bitwise_xor(position_ref[1], hop)
        for at, size, out, column in piece_parts:
            start = aligned(from_peer * columns_here[out] + column, size, HEAD_SIZE)
            copies.append(
                pltpu.make_async_copy(piece.at[:, at : at + size], outs[out].at[:, start], sem.at[len(copies)])
            )
            copies[-1].start()
    here = own_sources(mapping_ref, position_ref[0], block_count)
    share = block_count * block_rows // peers
    step = math.gcd(share, block_rows)
    for piece in range(share // step):
        block = lax.div(position_ref[1] * share + piece * step, block_rows)
        source = jnp.int32(-1)
        for slot in range(block_count):
            source = jnp.where(block == slot, here[slot], source)
        rows = slice(piece * step, (piece + 1) * step)
        for peer in range(peers):
            merged_ref[peer, rows, :] = jnp.where(source >= 0, spread_ref[peer, 0, rows, :], arrived_ref[peer, rows, :])
    for peer in range(peers):
        for at, size, out, column in parts:
            start = peer * columns_here[out] + column
            copies.append(
                pltpu.make_async_copy(
                    merged_ref.at[peer, :, at : at + size], outs[out].at[:, start : start + size], sem.at[len(copies)]
                )
            )
            copies[-1].start()
    for copy in copies:
        copy.wait()


def place_last(position, mapping, spread, arrived, parts, pieces, piece_parts, columns_here, held, block_count):
    peers, _, share, columns = spread.shape
    return pl.pallas_call(
        functools.partial(
            place_last_kernel, block_count, share * peers // block_count, peers, columns_here, parts, piece_parts
        ),
        in_specs=[IN_SMEM, IN_SMEM] + [IN_VMEM] * (2 + peers) + [ANYWHERE] * len(held),
        out_specs=[ANYWHERE] * len(held),
        out_shape=[jax.ShapeDtypeStruct(h.shape, h.dtype) for h in held],
        input_output_aliases={4 + peers + i: i for i in range(len(held))},
        scratch_shapes=[
            pltpu.VMEM((peers, share, columns), spread.dtype),
            pltpu.SemaphoreType.DMA((peers * (len(parts) + len(piece_parts)),)),
        ],
        compiler_params=pltpu.CompilerParams(vmem_limit_bytes=LITTLE_VMEM),
        cost_estimate=NO_COST,
    )(position, mapping, spread, arrived, *pieces, *held)


def joined_parts(parts):
    joined = []
    for at, size, out, column in parts:
        if joined and joined[-1][2] == out and joined[-1][0] + joined[-1][1] == at and joined[-1][3] + joined[-1][1] == column:
            joined[-1] = (joined[-1][0], joined[-1][1] + size, out, joined[-1][3])
        else:
            joined.append((at, size, out, column))
    return joined


def place_columns(position, pieces, places, columns_here, held, peers):
    rows, dtype = pieces[0][0].shape[-2], pieces[0][0].dtype
    flat = [p for chunk in pieces for p in chunk]
    count = peers * sum(len(parts) for parts in places)
    out_shape = [jax.ShapeDtypeStruct((rows, peers * c), dtype) for c in columns_here]
    return pl.pallas_call(
        functools.partial(place_kernel, peers, columns_here, places, len(held)),
        in_specs=[IN_SMEM] + [IN_VMEM] * len(flat) + [ANYWHERE] * len(held),
        out_specs=[ANYWHERE] * len(out_shape),
        out_shape=out_shape,
        input_output_aliases={1 + len(flat) + i: i for i in range(len(held))},
        scratch_shapes=[pltpu.SemaphoreType.DMA((count,))],
        compiler_params=pltpu.CompilerParams(vmem_limit_bytes=LITTLE_VMEM),
        cost_estimate=NO_COST,
    )(position, *flat, *held)


def plan_of(groups, repeats):
    lead, cut = max(1, 4 * repeats // 8), max(1, 4 * repeats // 8)
    heads = list(range(repeats))
    kernels = [(0, 0, lead, [heads[:lead]]), (0, lead, repeats - lead, [heads[: repeats - lead]])]
    for group in range(1, groups):
        kernels.append((group, 0, repeats, [heads[:cut], heads[cut:]]))
    for group in range(groups - 1):
        kernels[group + 2][3][0].append(keys_and_values(group))
    kernels[-1][3].append([keys_and_values(groups - 1)])
    return kernels


TOGETHER = 1


def on_device(queries, key_layout_rows, value_layout_rows, output_gradient, doc_starts, block_mapping):
    rows = queries.shape[0]
    block_count = doc_starts.shape[0]
    groups = key_layout_rows.shape[1] // HEAD_SIZE
    repeats = queries.shape[1] // key_layout_rows.shape[1]
    axis_length = lax.axis_size("ctx")
    half_axis = axis_length // 2
    peers = lax.axis_size("tensor")
    position = jnp.stack([lax.axis_index("ctx"), lax.axis_index("tensor")]).astype(jnp.int32)
    pairs = [(i, (i + half_axis) % axis_length) for i in range(axis_length)]

    carried, after, sent, landed = {}, key_layout_rows, [], []
    kernels = plan_of(groups, repeats)
    for number, (group, start, heads, sets) in enumerate(kernels):
        made, carried = grads_chunk(
            doc_starts, block_mapping, queries, output_gradient, key_layout_rows, value_layout_rows,
            after, carried, group * repeats + start, heads, group, sets, FULL_VMEM if number == 0 else SOME_VMEM,
        )
        after = made[0][0]
        for units, (own, send) in zip(sets, made):
            sent.append((group * repeats + start, units, own))
            if number < len(kernels) - 1 or len(sent) < sum(len(k[3]) for k in kernels):
                landed.append(lax.ppermute(send, "ctx", pairs))
    _, last_units, own = sent[-1]
    spread = spread_rows(position, block_mapping, own, send, landed[0], half_axis, block_count, peers)
    spread = lax.all_to_all(spread, "tensor", split_axis=0, concat_axis=0, tiled=True)
    last_arrived = lax.ppermute(spread[:, 1], "ctx", pairs)

    def parts_of(start, units):
        parts = []
        for unit in units:
            at = columns_before(units, unit)
            if unit >= 0:
                parts.append((at, HEAD_SIZE, 0, (start + unit) * HEAD_SIZE))
            else:
                parts.append((at, HEAD_SIZE, 1, group_of(unit) * HEAD_SIZE))
                parts.append((at + HEAD_SIZE, HEAD_SIZE, 2, group_of(unit) * HEAD_SIZE))
        return joined_parts(parts)

    order, pieces, places = [after], [], []
    chunks = list(zip(sent, landed))
    for chunk in [chunks[:TOGETHER]] + [[c] for c in chunks[TOGETHER:]]:
        sources = [(own, arrived) for (_, _, own), arrived in chunk]
        parts = sort_rows(position, block_mapping, sources, order, block_count, half_axis, peers)
        got = [parts[0]] + [
            lax.ppermute(parts[hop], "tensor", [(i, i ^ hop) for i in range(peers)]) for hop in range(1, peers)
        ]
        order = [got[0], got[1]] + (list(pieces[-1][2:]) if pieces else [])
        pieces.append(got)
        places.append([])
        before = 0
        for (start, units, own), _ in chunk:
            places[-1] += [(before + at, size, out, column) for at, size, out, column in parts_of(start, units)]
            before += own.shape[1]
        places[-1] = joined_parts(places[-1])
    columns_here = [queries.shape[1], key_layout_rows.shape[1], value_layout_rows.shape[1]]
    held = place_columns(position, pieces[:-1], places[:-1], columns_here, [], peers)
    parts = parts_of(0, last_units)
    return tuple(
        place_last(
            position, block_mapping, spread, last_arrived, parts, pieces[-1], places[-1], columns_here, held, block_count
        )
    )


def solution(mesh):
    return jax.shard_map(
        on_device,
        mesh=mesh,
        in_specs=(
            P("ctx", "tensor"),
            P("ctx", "tensor"),
            P("ctx", "tensor"),
            P("ctx", "tensor"),
            P("ctx"),
            P(),
        ),
        out_specs=(
            P(("ctx", "tensor"), None),
            P(("ctx", "tensor"), None),
            P(("ctx", "tensor"), None),
        ),
        check_vma=False,
    )
```

```python
import functools
import math

import jax
import jax.numpy as jnp
from jax import lax
from jax.experimental import pallas as pl
from jax.experimental.pallas import tpu as pltpu
from jax.sharding import PartitionSpec as P

HEAD_SIZE = 128
CAP = 2
HIDDEN = -1e30
FULL_VMEM, SOME_VMEM, LITTLE_VMEM = (60 << 20, 30 << 20, 8 << 20)
PACK = 4
NO_COST = pl.CostEstimate(flops=1000, bytes_accessed=1000, transcendentals=0)
IN_SMEM = pl.BlockSpec(memory_space=pltpu.SMEM)
IN_VMEM = pl.BlockSpec(memory_space=pltpu.VMEM)
ANYWHERE = pl.BlockSpec(memory_space=pl.ANY)


def contract(a, b, dims):
    return lax.dot_general(a, b, ((dims[:1], dims[1:]), ((), ())), preferred_element_type=jnp.float32)


def aligned(start, size, step):
    return pl.ds(pl.multiple_of(start, step), size)


def own_sources(mapping_ref, position, block_count):
    sources = [jnp.int32(-1)] * block_count
    for block in range(block_count):
        target = mapping_ref[position * block_count + block] - position * block_count
        for slot in range(block_count):
            sources[slot] = jnp.where(target == slot, block, sources[slot])
    return sources


def moved_blocks(mapping_ref, position, block_count):
    moved = [jnp.int32(0)] * CAP
    seen = jnp.int32(0)
    for block in range(block_count):
        target = mapping_ref[position * block_count + block] - position * block_count
        leaves = (target < 0) | (target >= block_count)
        for slot in range(CAP):
            moved[slot] = jnp.where(leaves & (seen <= slot), block, moved[slot])
        seen = seen + jnp.where(leaves, 1, 0)
    return moved


def heads_gradients(q_ref, g_ref, k_ref, v_ref, bias_ref, columns, block_count, block_rows):
    rate = HEAD_SIZE ** (-0.5) * math.log2(math.e)
    weights_low, dscores, query_pieces = [], [], []
    for block in range(block_count):
        rows = slice(block * block_rows, (block + 1) * block_rows)
        width = (block + 1) * block_rows
        q = jnp.concatenate([q_ref[rows, c] for c in columns], axis=0)
        g = jnp.concatenate([g_ref[rows, c] for c in columns], axis=0)
        k, v = k_ref[:width, :], v_ref[:width, :]
        bias = jnp.concatenate([bias_ref[:width, rows]] * len(columns), axis=1)
        scores = contract(k, q, (1, 1)) + bias
        top = jnp.max(scores, axis=0, keepdims=True)
        weights = jnp.exp2((scores - top) * rate)
        dprobs = contract(v, g, (1, 1))
        share = 1.0 / jnp.sum(weights, axis=0, keepdims=True)
        delta = jnp.sum(weights * dprobs, axis=0, keepdims=True) * share
        weights = weights * share
        weights_low.append(weights.astype(jnp.bfloat16))
        dscores.append((weights * (dprobs - delta)).astype(jnp.bfloat16))
        query_pieces.append((contract(dscores[-1], k, (0, 0)) * HEAD_SIZE ** (-0.5)).astype(jnp.bfloat16))
    return query_pieces, dscores, weights_low


def pairs_of(refs):
    return list(zip(refs[::2], refs[1::2]))


def grads_kernel(block_count, block_rows, group, first, keeps, held, heads, sets, *refs):
    starts_ref, mapping_ref, q_ref, g_ref, k_ref, v_ref, _, *refs = refs
    sums, refs = dict(zip(held, pairs_of(refs[: 2 * len(held)]))), refs[2 * len(held) :]
    outs, refs = pairs_of(refs[: 2 * len(sets)]), refs[2 * len(sets) :]
    if keeps:
        key_out, value_out, *refs = refs
    bias_ref, low_ref, key_acc, value_acc = refs
    position = lax.axis_index("ctx")
    rows = block_count * block_rows

    document_row = jnp.int32(0)
    for block in range(block_count):
        document_row = jnp.where(starts_ref[block] != 0, block * block_rows, document_row)
        width = (block + 1) * block_rows
        at_key = lax.broadcasted_iota(jnp.int32, (width, block_rows), 0)
        at_row = lax.broadcasted_iota(jnp.int32, (width, block_rows), 1) + block * block_rows
        visible = (at_key <= at_row) & (at_key >= document_row)
        bias_ref[:width, block * block_rows : width] = jnp.where(visible, 0.0, HIDDEN)
    if first:
        key_acc[...] = jnp.zeros_like(key_acc)
        value_acc[...] = jnp.zeros_like(value_acc)
    else:
        key_acc[...] = sums[group][0][...]
        value_acc[...] = sums[group][1][...]
    sums[group] = (key_acc, value_acc)

    owned = [jnp.maximum(source, 0) for source in own_sources(mapping_ref, position, block_count)]
    moved = moved_blocks(mapping_ref, position, block_count)

    def put(own_ref, send_ref, at):
        columns = slice(at * HEAD_SIZE, (at + 1) * HEAD_SIZE)
        for slot, source in enumerate(owned):
            own_ref[slot * block_rows : (slot + 1) * block_rows, columns] = low_ref[
                aligned(source * block_rows, block_rows, block_rows), :
            ]
        for slot, source in enumerate(moved):
            send_ref[slot * block_rows : (slot + 1) * block_rows, columns] = low_ref[
                aligned(source * block_rows, block_rows, block_rows), :
            ]

    places = {}
    for units, (own_ref, send_ref) in zip(sets, outs):
        for unit in units:
            places[unit] = (own_ref, send_ref, columns_before(units, unit) // HEAD_SIZE)
    for head in range(0, heads, PACK):
        packed = range(head, min(head + PACK, heads))
        columns = [slice(h * HEAD_SIZE, (h + 1) * HEAD_SIZE) for h in packed]
        query_pieces, dscores, weights_low = heads_gradients(
            q_ref, g_ref, k_ref, v_ref, bias_ref, columns, block_count, block_rows
        )
        stacked = lambda ref, block: [ref[b * block_rows : (b + 1) * block_rows, c] for b in range(block, block_count) for c in columns]
        for block in range(block_count):
            seen = slice(block * block_rows, (block + 1) * block_rows)
            joined = lambda pieces: jnp.concatenate([p[seen, :] for p in pieces[block:]], axis=1)
            value_acc[seen, :] += contract(joined(weights_low), jnp.concatenate(stacked(g_ref, block), axis=0), (1, 0))
            key_acc[seen, :] += contract(joined(dscores), jnp.concatenate(stacked(q_ref, block), axis=0), (1, 0))
        for index, h in enumerate(packed):
            for block in range(block_count):
                low_ref[block * block_rows : (block + 1) * block_rows, :] = query_pieces[block][
                    index * block_rows : (index + 1) * block_rows, :
                ]
            put(*places[h])
    for unit, (own_ref, send_ref, at) in places.items():
        if unit < 0:
            key_sum, value_sum = sums[group_of(unit)]
            low_ref[...] = (key_sum[...] * HEAD_SIZE ** (-0.5)).astype(jnp.bfloat16)
            put(own_ref, send_ref, at)
            low_ref[...] = value_sum[...].astype(jnp.bfloat16)
            put(own_ref, send_ref, at + 1)
    if keeps:
        key_out[...] = key_acc[...]
        value_out[...] = value_acc[...]


def keys_and_values(group):
    return -1 - group


def group_of(unit):
    return -1 - unit


def columns_before(units, unit=None):
    ahead = units if unit is None else units[: units.index(unit)]
    return sum(HEAD_SIZE if u >= 0 else 2 * HEAD_SIZE for u in ahead)


def grads_chunk(
    starts, mapping, queries, gradient, keys, values, after, carried, start_head, heads, group, sets,
    vmem=FULL_VMEM,
):
    rows = queries.shape[0]
    block_count = starts.shape[0]
    block_rows = rows // block_count
    sent_groups = [group_of(u) for units in sets for u in units if u < 0]
    held = [g for g in carried if g == group or g in sent_groups]
    keeps = group not in sent_groups
    whole = lambda r, c: pl.BlockSpec((r, c), lambda i: (0, 0))
    cut = pl.BlockSpec((pl.Element(rows), pl.Element(heads * HEAD_SIZE)), lambda i: (0, start_head * HEAD_SIZE))
    group_spec = pl.BlockSpec((rows, HEAD_SIZE), lambda i: (0, group))
    running = jax.ShapeDtypeStruct((rows, HEAD_SIZE), jnp.float32)
    out_shape = []
    for units in sets:
        out_shape.append(jax.ShapeDtypeStruct((rows, columns_before(units)), jnp.bfloat16))
        out_shape.append(jax.ShapeDtypeStruct((CAP * block_rows, columns_before(units)), jnp.bfloat16))
    if keeps:
        out_shape += [running, running]
    out = pl.pallas_call(
        functools.partial(grads_kernel, block_count, block_rows, group, group not in held, keeps, held, heads, sets),
        grid=(1,),
        in_specs=[IN_SMEM] * 2
        + [cut, cut, group_spec, group_spec, ANYWHERE]
        + [whole(rows, HEAD_SIZE)] * (2 * len(held)),
        out_specs=[whole(*s.shape) for s in out_shape],
        out_shape=out_shape,
        scratch_shapes=[
            pltpu.VMEM((rows, rows), jnp.float32),
            pltpu.VMEM((rows, HEAD_SIZE), jnp.bfloat16),
            pltpu.VMEM((rows, HEAD_SIZE), jnp.float32),
            pltpu.VMEM((rows, HEAD_SIZE), jnp.float32),
        ],
        compiler_params=pltpu.CompilerParams(vmem_limit_bytes=vmem),
        cost_estimate=NO_COST,
    )(starts, mapping, queries, gradient, keys, values, after, *(x for g in held for x in carried[g]))
    carried = {g: sums for g, sums in carried.items() if g not in held}
    if keeps:
        carried[group] = tuple(out[2 * len(sets) :])
    return pairs_of(out[: 2 * len(sets)]), carried


def sort_kernel(block_count, block_rows, half_axis, peers, widths, position_ref, mapping_ref, *refs):
    sources, outs = pairs_of(refs[: 2 * len(widths)]), refs[-peers:]
    at, peer = position_ref[0], position_ref[1]
    partner = lax.rem(at + half_axis, 2 * half_axis)
    arrived_slot = [jnp.int32(-1)] * block_count
    for index, block in enumerate(moved_blocks(mapping_ref, partner, block_count)):
        target = mapping_ref[partner * block_count + block] - at * block_count
        for slot in range(block_count):
            arrived_slot[slot] = jnp.where(target == slot, index, arrived_slot[slot])
    share = block_count * block_rows // peers
    step = math.gcd(share, block_rows)
    for hop, out_ref in enumerate(outs):
        to_peer = jnp.bitwise_xor(peer, hop)
        for piece in range(share // step):
            row = to_peer * share + piece * step
            block = lax.div(row, block_rows)
            slot = jnp.int32(-1)
            for b in range(block_count):
                slot = jnp.where(block == b, arrived_slot[b], slot)
            at_pair = jnp.maximum(slot, 0) * block_rows + lax.rem(row, block_rows)
            column = 0
            for (own_ref, arrived_ref), width in zip(sources, widths):
                from_own = own_ref[aligned(row, step, step), :]
                from_pair = arrived_ref[aligned(at_pair, step, step), :]
                out_ref[piece * step : (piece + 1) * step, column : column + width] = jnp.where(
                    slot >= 0, from_pair, from_own
                )
                column += width


def sort_rows(position, mapping, sources, after, block_count, half_axis, peers):
    rows = sources[0][0].shape[0]
    widths = [own.shape[1] for own, _ in sources]
    out = jax.ShapeDtypeStruct((rows // peers, sum(widths)), sources[0][0].dtype)
    return pl.pallas_call(
        functools.partial(sort_kernel, block_count, rows // block_count, half_axis, peers, widths),
        in_specs=[IN_SMEM, IN_SMEM] + [IN_VMEM] * (2 * len(sources)) + [ANYWHERE] * len(after),
        out_specs=[IN_VMEM] * peers,
        out_shape=[out] * peers,
        compiler_params=pltpu.CompilerParams(vmem_limit_bytes=LITTLE_VMEM),
        cost_estimate=NO_COST,
    )(position, mapping, *(x for source in sources for x in source), *after)


def place_kernel(peers, columns_here, places, held, position_ref, *refs):
    pieces = list(refs)
    outs, sem = refs[-len(columns_here) - 1 : -1], refs[-1]
    peer = position_ref[1]
    copies = []
    for parts in places:
        for hop in range(peers):
            from_peer = jnp.bitwise_xor(peer, hop)
            piece = pieces.pop(0)
            for at, size, out, column in parts:
                copies.append(
                    pltpu.make_async_copy(
                        piece.at[:, at : at + size],
                        outs[out].at[:, aligned(from_peer * columns_here[out] + column, size, HEAD_SIZE)],
                        sem.at[len(copies)],
                    )
                )
                copies[-1].start()
    for copy in copies:
        copy.wait()


def spread_kernel(block_count, block_rows, half_axis, peers, position_ref, mapping_ref, own_ref, send_ref, _, out_ref):
    at = position_ref[0]
    partner = lax.rem(at + half_axis, 2 * half_axis)
    send_slot = [jnp.int32(0)] * block_count
    for index, block in enumerate(moved_blocks(mapping_ref, at, block_count)):
        target = mapping_ref[at * block_count + block] - partner * block_count
        for slot in range(block_count):
            send_slot[slot] = jnp.where(target == slot, index, send_slot[slot])
    share = block_count * block_rows // peers
    step = math.gcd(share, block_rows)
    for peer in range(peers):
        out_ref[peer, 0] = own_ref[peer * share : (peer + 1) * share, :]
        for piece in range(share // step):
            row = peer * share + piece * step
            at_send = send_slot[row // block_rows] * block_rows + row % block_rows
            out_ref[peer, 1, piece * step : (piece + 1) * step, :] = send_ref[aligned(at_send, step, step), :]


def spread_rows(position, mapping, own, send, after, half_axis, block_count, peers):
    rows, columns = own.shape
    return pl.pallas_call(
        functools.partial(spread_kernel, block_count, rows // block_count, half_axis, peers),
        in_specs=[IN_SMEM, IN_SMEM, IN_VMEM, IN_VMEM, ANYWHERE],
        out_specs=IN_VMEM,
        out_shape=jax.ShapeDtypeStruct((peers, 2, rows // peers, columns), own.dtype),
        compiler_params=pltpu.CompilerParams(vmem_limit_bytes=LITTLE_VMEM),
        cost_estimate=NO_COST,
    )(position, mapping, own, send, after)


def place_last_kernel(block_count, block_rows, peers, columns_here, parts, piece_parts, *refs):
    position_ref, mapping_ref, spread_ref, arrived_ref, *refs = refs
    pieces = refs[:peers]
    outs, merged_ref, sem = refs[-len(columns_here) - 2 : -2], refs[-2], refs[-1]
    copies = []
    for hop, piece in enumerate(pieces):
        from_peer = jnp.bitwise_xor(position_ref[1], hop)
        for at, size, out, column in piece_parts:
            start = aligned(from_peer * columns_here[out] + column, size, HEAD_SIZE)
            copies.append(
                pltpu.make_async_copy(piece.at[:, at : at + size], outs[out].at[:, start], sem.at[len(copies)])
            )
            copies[-1].start()
    here = own_sources(mapping_ref, position_ref[0], block_count)
    share = block_count * block_rows // peers
    step = math.gcd(share, block_rows)
    for piece in range(share // step):
        block = lax.div(position_ref[1] * share + piece * step, block_rows)
        source = jnp.int32(-1)
        for slot in range(block_count):
            source = jnp.where(block == slot, here[slot], source)
        rows = slice(piece * step, (piece + 1) * step)
        for peer in range(peers):
            merged_ref[peer, rows, :] = jnp.where(source >= 0, spread_ref[peer, 0, rows, :], arrived_ref[peer, rows, :])
    for peer in range(peers):
        for at, size, out, column in parts:
            start = peer * columns_here[out] + column
            copies.append(
                pltpu.make_async_copy(
                    merged_ref.at[peer, :, at : at + size], outs[out].at[:, start : start + size], sem.at[len(copies)]
                )
            )
            copies[-1].start()
    for copy in copies:
        copy.wait()


def place_last(position, mapping, spread, arrived, parts, pieces, piece_parts, columns_here, held, block_count):
    peers, _, share, columns = spread.shape
    return pl.pallas_call(
        functools.partial(
            place_last_kernel, block_count, share * peers // block_count, peers, columns_here, parts, piece_parts
        ),
        in_specs=[IN_SMEM, IN_SMEM] + [IN_VMEM] * (2 + peers) + [ANYWHERE] * len(held),
        out_specs=[ANYWHERE] * len(held),
        out_shape=[jax.ShapeDtypeStruct(h.shape, h.dtype) for h in held],
        input_output_aliases={4 + peers + i: i for i in range(len(held))},
        scratch_shapes=[
            pltpu.VMEM((peers, share, columns), spread.dtype),
            pltpu.SemaphoreType.DMA((peers * (len(parts) + len(piece_parts)),)),
        ],
        compiler_params=pltpu.CompilerParams(vmem_limit_bytes=LITTLE_VMEM),
        cost_estimate=NO_COST,
    )(position, mapping, spread, arrived, *pieces, *held)


def joined_parts(parts):
    joined = []
    for at, size, out, column in parts:
        if joined and joined[-1][2] == out and joined[-1][0] + joined[-1][1] == at and joined[-1][3] + joined[-1][1] == column:
            joined[-1] = (joined[-1][0], joined[-1][1] + size, out, joined[-1][3])
        else:
            joined.append((at, size, out, column))
    return joined


def place_columns(position, pieces, places, columns_here, held, peers):
    rows, dtype = pieces[0][0].shape[-2], pieces[0][0].dtype
    flat = [p for chunk in pieces for p in chunk]
    count = peers * sum(len(parts) for parts in places)
    out_shape = [jax.ShapeDtypeStruct((rows, peers * c), dtype) for c in columns_here]
    return pl.pallas_call(
        functools.partial(place_kernel, peers, columns_here, places, len(held)),
        in_specs=[IN_SMEM] + [IN_VMEM] * len(flat) + [ANYWHERE] * len(held),
        out_specs=[ANYWHERE] * len(out_shape),
        out_shape=out_shape,
        input_output_aliases={1 + len(flat) + i: i for i in range(len(held))},
        scratch_shapes=[pltpu.SemaphoreType.DMA((count,))],
        compiler_params=pltpu.CompilerParams(vmem_limit_bytes=LITTLE_VMEM),
        cost_estimate=NO_COST,
    )(position, *flat, *held)


def plan_of(groups, repeats):
    lead, cut = max(1, 4 * repeats // 8), max(1, 4 * repeats // 8)
    heads = list(range(repeats))
    kernels = [(0, 0, lead, [heads[:lead]]), (0, lead, repeats - lead, [heads[: repeats - lead]])]
    for group in range(1, groups):
        kernels.append((group, 0, repeats, [heads[:cut], heads[cut:]]))
    for group in range(groups - 1):
        kernels[group + 2][3][0].append(keys_and_values(group))
    kernels[-1][3].append([keys_and_values(groups - 1)])
    return kernels


TOGETHER = 1


def on_device(queries, key_layout_rows, value_layout_rows, output_gradient, doc_starts, block_mapping):
    rows = queries.shape[0]
    block_count = doc_starts.shape[0]
    groups = key_layout_rows.shape[1] // HEAD_SIZE
    repeats = queries.shape[1] // key_layout_rows.shape[1]
    axis_length = lax.axis_size("ctx")
    half_axis = axis_length // 2
    peers = lax.axis_size("tensor")
    position = jnp.stack([lax.axis_index("ctx"), lax.axis_index("tensor")]).astype(jnp.int32)
    pairs = [(i, (i + half_axis) % axis_length) for i in range(axis_length)]

    carried, after, sent, landed = {}, key_layout_rows, [], []
    kernels = plan_of(groups, repeats)
    for number, (group, start, heads, sets) in enumerate(kernels):
        made, carried = grads_chunk(
            doc_starts, block_mapping, queries, output_gradient, key_layout_rows, value_layout_rows,
            after, carried, group * repeats + start, heads, group, sets, FULL_VMEM if number < 2 else SOME_VMEM,
        )
        after = made[0][0]
        for units, (own, send) in zip(sets, made):
            sent.append((group * repeats + start, units, own))
            if number < len(kernels) - 1 or len(sent) < sum(len(k[3]) for k in kernels):
                landed.append(lax.ppermute(send, "ctx", pairs))
    _, last_units, own = sent[-1]
    spread = spread_rows(position, block_mapping, own, send, landed[0], half_axis, block_count, peers)
    spread = lax.all_to_all(spread, "tensor", split_axis=0, concat_axis=0, tiled=True)
    last_arrived = lax.ppermute(spread[:, 1], "ctx", pairs)

    def parts_of(start, units):
        parts = []
        for unit in units:
            at = columns_before(units, unit)
            if unit >= 0:
                parts.append((at, HEAD_SIZE, 0, (start + unit) * HEAD_SIZE))
            else:
                parts.append((at, HEAD_SIZE, 1, group_of(unit) * HEAD_SIZE))
                parts.append((at + HEAD_SIZE, HEAD_SIZE, 2, group_of(unit) * HEAD_SIZE))
        return joined_parts(parts)

    order, pieces, places = [after], [], []
    chunks = list(zip(sent, landed))
    for chunk in [chunks[:TOGETHER]] + [[c] for c in chunks[TOGETHER:]]:
        sources = [(own, arrived) for (_, _, own), arrived in chunk]
        if len(pieces) == 2:
            order = order + [spread]
        parts = sort_rows(position, block_mapping, sources, order, block_count, half_axis, peers)
        got = [parts[0]] + [
            lax.ppermute(parts[hop], "tensor", [(i, i ^ hop) for i in range(peers)]) for hop in range(1, peers)
        ]
        order = [got[0], got[1]] + (list(pieces[-1][2:]) if pieces else [])
        pieces.append(got)
        places.append([])
        before = 0
        for (start, units, own), _ in chunk:
            places[-1] += [(before + at, size, out, column) for at, size, out, column in parts_of(start, units)]
            before += own.shape[1]
        places[-1] = joined_parts(places[-1])
    columns_here = [queries.shape[1], key_layout_rows.shape[1], value_layout_rows.shape[1]]
    held = place_columns(position, pieces[:-1], places[:-1], columns_here, [], peers)
    parts = parts_of(0, last_units)
    return tuple(
        place_last(
            position, block_mapping, spread, last_arrived, parts, pieces[-1], places[-1], columns_here, held, block_count
        )
    )


def solution(mesh):
    return jax.shard_map(
        on_device,
        mesh=mesh,
        in_specs=(
            P("ctx", "tensor"),
            P("ctx", "tensor"),
            P("ctx", "tensor"),
            P("ctx", "tensor"),
            P("ctx"),
            P(),
        ),
        out_specs=(
            P(("ctx", "tensor"), None),
            P(("ctx", "tensor"), None),
            P(("ctx", "tensor"), None),
        ),
        check_vma=False,
    )
```
